512 devices in a mesh: dp: 32 (over z, x_hi), ctx: 16 (over x_lo, y, core).
Axes of the slice: x: 4 (x_hi: 2, x_lo: 2; x = x_hi * 2 + x_lo), y: 4, z: 16, core: 2. Of those that a mesh axis runs over, the one named last changes fastest.
Arguments:
- inputs: bfloat16 [32, 2048, 4096], P('dp', 'ctx'), may hold values from -6 to 6
- letters: int32 [32, 2048], P('dp', 'ctx'), may hold values from 0 to 3
- letter_table: bfloat16 [3, 4, 4096], replicated, may hold values from -3 to 3
- short_taps: bfloat16 [3, 3, 4096], replicated, may hold values from -3 to 3
- residues: float32 [4096, 16], P('ctx'), may hold values from -1.5 to 1.5
- decay_rate: float32 [4096, 16], P('ctx'), may hold values from 2.4414063e-05 to 0.024414062
- cotangent: bfloat16 [32, 2048, 4096], P('dp', 'ctx'), may hold values from -6 to 6
Outputs:
- input_grad: bfloat16 [32, 2048, 4096], P('dp', 'ctx')
- taps_grad: float32 [3, 3, 4096], P(None, None, 'ctx')
- table_grad: float32 [3, 4, 4096], P(None, None, 'ctx')
- residue_grad: float32 [4096, 16], P('ctx')
- decay_grad: float32 [4096, 16], P('ctx')
The draws below stay inside these ranges and needn't reach their ends.
All inputs are finite; a program needn't handle non-finite values.
Results may differ from the reference program's by a relative error of at most 0.005.
Values may be sent and summed in bfloat16 or wider, within the bound.
A program may use at most 128 MiB of HBM per device.

```python
import math
import jax
import jax.numpy as jnp
from jax import lax

D = 4096
MODES = 16
BATCH = 32
LEN = 2048


def set_ends(values, own_key, low, top_value):
    extent = values.shape
    place = [jax.random.randint(jax.random.fold_in(own_key, axis), (), 0, extent[axis]) for axis in range(len(extent))]
    values = values.at[tuple(place)].set(low)
    longest = extent.index(max(extent))
    place[longest] = (place[longest] + 1) % extent[longest]
    return values.at[tuple(place)].set(top_value)


def spiked(values, key, source, target, parts, factor):
    def block_of(position):
        return (jnp.arange(values.shape[position]) // (values.shape[position] // parts)).reshape((-1,) + (1,) * (values.ndim - 1 - position))

    first = jax.random.permutation(key, parts)[block_of(target)]
    second = (block_of(target) + parts // 2) % parts
    return jnp.where((block_of(source) == first) | (block_of(source) == second), factor * values, values)


def steps_of(key, dims, pieces, smallest, top_value):
    loudness = 1.0
    for position, blocks in pieces:
        draws = jax.random.uniform(jax.random.fold_in(jax.random.fold_in(key, 6), position), (blocks,), jnp.float32, smallest / len(pieces), top_value / len(pieces))
        loudness = loudness * jnp.repeat(jnp.exp(draws), dims[position] // blocks).reshape((-1,) + (1,) * (len(dims) - 1 - position))
    return loudness


def noise(own_key, extent, spread, most, cuts=(), held_as=jnp.bfloat16):
    drawn = jax.random.normal(own_key, extent, jnp.float32) * spread
    if len(cuts) > 0:
        drawn = steps_of(own_key, extent, cuts, -0.22, 0.18) * drawn
    return jnp.clip(drawn, min=-most, max=most).astype(held_as)


def gaussian_with(own_key, extent, deviation, reach, split, heavy, kind=jnp.bfloat16):
    drawn = deviation * jax.random.normal(own_key, extent, jnp.float32)
    if split:
        drawn = drawn * steps_of(own_key, extent, split, -0.22, 0.18)
    return jnp.clip(spiked(drawn, jax.random.fold_in(own_key, 3), *heavy), -reach, reach).astype(kind)


def setup_inputs(seed: int = 0) -> dict:
    key_of = jax.random.split(jax.random.key(seed), 8)
    inputs = noise(key_of[0], (BATCH, LEN, D), 1.0, 6.0, ((0, 32), (1, 16)))
    letters = set_ends(jax.random.randint(key_of[1], (BATCH, LEN), 0, 4), jax.random.fold_in(key_of[1], 1), 0, 3).astype(jnp.int32)
    letter_table = noise(key_of[2], (3, 4, D), 0.5, 3.0)
    short_taps = noise(key_of[3], (3, 3, D), 0.6, 3.0)
    residues = noise(key_of[4], (D, MODES), 0.25, 1.5, ((0, 16),), jnp.float32)
    decay_rate = jnp.clip(jnp.exp(math.log(0.024414062) - 6.9077553 * jax.random.uniform(key_of[5], (D, MODES), jnp.float32) ** steps_of(key_of[5], (D, MODES), ((0, 16),), -0.2, 0.2)), 2.441406286379788e-05, 0.024414062)
    cotangent = gaussian_with(key_of[6], (BATCH, LEN, D), 1.0, 6.0, ((0, 32), (1, 16)), (0, 2, 32, 2.75))
    return {"inputs": inputs, "letters": letters, "letter_table": letter_table, "short_taps": short_taps, "residues": residues, "decay_rate": decay_rate, "cotangent": cotangent}


def filter_taps(residues, decay_rate, length):
    positions = jnp.arange(length, dtype=jnp.float32)[:, None, None]
    weight = residues * jnp.sqrt(-jnp.expm1(-2.0 * decay_rate))
    return lax.optimization_barrier(jnp.sum(weight[None] * jnp.exp(-decay_rate[None] * positions), axis=2))

def shifted(row_block, offset):
    zeros_head = jnp.zeros((offset,) + row_block.shape[1:], row_block.dtype)
    return jnp.concatenate([zeros_head, row_block[:row_block.shape[0] - offset]], axis=0)

def reference(inputs, letters, letter_table, short_taps, residues, decay_rate, cotangent):
    weight_values = short_taps.astype(jnp.float32)
    embedding_matrix = letter_table.astype(jnp.float32)

    def make_filter(residue_part, decay_part):
        return filter_taps(residue_part, decay_part, LEN)
    filter_rows, filter_pull = jax.vjp(make_filter, residues, decay_rate)
    spec_filter = jnp.fft.rfft(filter_rows, n=2 * LEN, axis=0)

    def one_sequence(totals, slices):
        rows_in, letter_ids, grad_out = slices
        base_rows = rows_in.astype(jnp.float32)
        delayed_input = jnp.stack([base_rows, shifted(base_rows, 1), shifted(base_rows, 2)])
        indicator_rows = (letter_ids[:, None] == jnp.arange(4, dtype=jnp.int32)[None, :]).astype(jnp.float32)
        feature_rows = jnp.einsum('nby,buy->nuy', weight_values, delayed_input)
        feature_rows = feature_rows + jnp.einsum('bi,pih->pbh', indicator_rows, embedding_matrix, precision=lax.Precision.HIGHEST)
        query_rows, key_rows, value_rows = (feature_rows[0], feature_rows[1], feature_rows[2])
        grad_rows = grad_out.astype(jnp.float32)
        mixed_rows = (key_rows * value_rows).astype(jnp.bfloat16)
        gated_rows = (grad_rows * query_rows).astype(jnp.bfloat16)
        spec_mixed = jnp.fft.rfft(mixed_rows.astype(jnp.float32), n=2 * LEN, axis=0)
        spec_gated = jnp.fft.rfft(gated_rows.astype(jnp.float32), n=2 * LEN, axis=0)
        conv_rows = jnp.fft.irfft(spec_filter * spec_mixed, n=2 * LEN, axis=0)[:LEN].astype(jnp.bfloat16)
        back_rows = jnp.fft.irfft(jnp.conj(spec_filter) * spec_gated, n=2 * LEN, axis=0)[:LEN].astype(jnp.bfloat16)
        filter_grad = jnp.fft.irfft(jnp.conj(spec_mixed) * spec_gated, n=2 * LEN, axis=0)[:LEN]
        back_f32 = back_rows.astype(jnp.float32)
        feature_gradient = jnp.stack([grad_rows * conv_rows.astype(jnp.float32), back_f32 * value_rows, back_f32 * key_rows])
        taps_gradient_piece = jnp.einsum('pva,nva->pna', feature_gradient, delayed_input)
        table_gradient_piece = jnp.einsum('nx,rnw->rxw', indicator_rows, feature_gradient, precision=lax.Precision.HIGHEST)
        ahead_rows = jnp.concatenate([feature_gradient, jnp.zeros((3, 2, D), jnp.float32)], axis=1)
        input_sum = jnp.zeros((LEN, D), jnp.float32)
        for offset in range(3):
            input_sum = input_sum + lax.optimization_barrier(jnp.sum(weight_values[:, offset, None, :] * ahead_rows[:, offset:offset + LEN], axis=0))
        new_totals = (totals[0] + taps_gradient_piece, totals[1] + table_gradient_piece, totals[2] + filter_grad)
        return (new_totals, input_sum.astype(jnp.bfloat16))
    start_totals = (jnp.zeros((3, 3, D), jnp.float32), jnp.zeros((3, 4, D), jnp.float32), jnp.zeros((LEN, D), jnp.float32))
    totals, input_grad = lax.scan(one_sequence, start_totals, (inputs, letters, cotangent))
    residue_grad, decay_grad = filter_pull(totals[2])
    return (input_grad, totals[0], totals[1], residue_grad, decay_grad)
```

```python
import functools

import jax
import jax.numpy as jnp
import numpy as np
from jax import lax
from jax.experimental import pallas as pl
from jax.experimental.pallas import tpu as pltpu
from jax.sharding import PartitionSpec as P

MESH = pl.DeviceIdType.MESH
F32 = jnp.float32
BF16 = jnp.bfloat16
NODES = 16
MODES = 16
ROWS = 16
PIECE = 24
PAY = 64


def split(values):
    high = values.astype(jnp.bfloat16)
    low = (values - high.astype(np.float64)).astype(jnp.bfloat16)
    return high, low


def tables(span):
    half = span / 2
    centre = (span - 1) / 2
    angles = np.pi * (2 * np.arange(NODES) + 1) / (2 * NODES)
    nodes = centre + half * np.cos(angles)
    places = np.arange(span)
    interp = np.ones((span, NODES))
    for k in range(NODES):
        for other in range(NODES):
            if other != k:
                interp[:, k] *= (places - nodes[other]) / (nodes[k] - nodes[other])
    theta = 2 * np.pi * (np.arange(span) + 0.5) / (2 * span)
    phase = theta[:, None] * places[None, :]
    forward = np.concatenate([np.cos(phase), -np.sin(phase)], axis=0)
    inverse = np.concatenate([np.cos(phase.T), -np.sin(phase.T)], axis=1) / span
    f_hi, f_lo = split(forward)
    l_hi, l_lo = split(interp)
    w_hi, w_lo = split(forward @ interp)
    m_hi, m_lo = split(interp.T @ inverse)
    return dict(
        nodes=nodes,
        forward=np.concatenate(
            [np.concatenate([f_hi, f_lo], axis=1), np.concatenate([l_hi.T, l_lo.T], axis=1)], axis=0
        ),
        inverse=inverse.astype(jnp.bfloat16),
        spread=np.concatenate([l_hi, l_lo], axis=1),
        response=np.concatenate([w_hi, w_lo], axis=1),
        gather=np.concatenate([m_hi, m_lo], axis=0),
    )


def dot(left, right):
    return jnp.dot(left, right, preferred_element_type=F32)


def kernel(
    n,
    near,
    groups,
    span,
    chans,
    nodes,
    x_ref,
    letters_ref,
    table_ref,
    taps_ref,
    res_ref,
    decay_ref,
    cot_ref,
    fwd_ref,
    inv_ref,
    spread_ref,
    resp_ref,
    gather_ref,
    node_ref,
    grad_ref,
    taps_out,
    table_out,
    res_out,
    decay_out,
    xs,
    key_s,
    value_s,
    spec_m,
    spec_g,
    near_c,
    near_b,
    letter_s,
    hot_s,
    hot_t,
    tbl_s,
    tap_s,
    prod_s,
    far_s,
    fg_s,
    w_s,
    tail_s,
    e_s,
    ep_s,
    gt_s,
    gr_s,
    a_s,
    r_s,
    s_s,
    u_s,
    al_s,
    rl_s,
    row_s,
    par_s,
    halo_stage,
    halo_recv,
    edge_stage,
    edge_recv,
    hn_stage,
    hn_recv,
    pq_stage,
    pq_recv,
    fgn_stage,
    fgn_recv,
    yz_stage,
    yz_recv,
    piece_stage,
    piece_recv,
    pay,
    one_recv,
    two_recv,
    three_recv,
    edge_sem,
    hn_send,
    hn_sem,
    pq_send,
    pq_sem,
    fgn_send,
    fgn_sem,
    yz_send,
    yz_sem,
    piece_send,
    piece_sem,
    one_send,
    one_sem,
    two_send,
    two_sem,
    three_send,
    three_sem,
):
    me = lax.axis_index("ctx")
    seq = lax.axis_index("dp")
    mine, block = lax.rem(seq, near), seq // near
    ahead, behind = lax.rem(me + 1, n), lax.rem(me + n - 1, n)
    chunk = PAY // near

    def lanes(d):
        return pl.ds(pl.multiple_of(d * chans, chans), chans)

    def to_ctx(source, target, send, recv, d):
        return pltpu.make_async_remote_copy(
            src_ref=source, dst_ref=target, send_sem=send, recv_sem=recv,
            device_id=(seq, d), device_id_type=MESH,
        )

    def to_dp(source, target, send, recv, p):
        return pltpu.make_async_remote_copy(
            src_ref=source, dst_ref=target, send_sem=send, recv_sem=recv,
            device_id=(p, me), device_id_type=MESH,
        )

    barrier = pltpu.get_barrier_semaphore()

    def greet_ctx(r, carry):
        pl.semaphore_signal(barrier, inc=1, device_id=(seq, lax.rem(me + r, n)), device_id_type=MESH)
        return carry

    def greet_near(r, carry):
        peer = block * near + lax.rem(mine + r, near)
        pl.semaphore_signal(barrier, inc=1, device_id=(peer, me), device_id_type=MESH)
        return carry

    def greet_far(r, carry):
        peer = lax.rem(block + r, groups) * near + mine
        pl.semaphore_signal(barrier, inc=1, device_id=(peer, me), device_id_type=MESH)
        return carry

    lax.fori_loop(1, n, greet_ctx, 0)
    lax.fori_loop(1, near, greet_near, 0)
    lax.fori_loop(1, groups, greet_far, 0)

    def widen(g, carry):
        at = lanes(g)
        xs[8:, at] = x_ref[:, at].astype(F32)
        tap_s[0:3, at] = taps_ref[0, :, at].astype(F32)
        tap_s[3:6, at] = taps_ref[1, :, at].astype(F32)
        tap_s[6:9, at] = taps_ref[2, :, at].astype(F32)
        rows = [table_ref[s, :, at].astype(F32) for s in range(3)]
        rows.append(jnp.zeros((4, chans), F32))
        tbl_s[:, at] = jnp.concatenate(rows, axis=0).astype(BF16)
        return carry

    lax.fori_loop(0, n, widen, 0)
    halo_stage[...] = xs[span + 6 : span + 8, :]

    codes = jnp.concatenate([letters_ref[...] + 4 * s for s in range(3)], axis=1)
    hot = (lax.broadcasted_iota(jnp.int32, (128, 3 * span), 0) == codes).astype(F32)
    hot_t[...] = hot[:ROWS].astype(BF16)
    hot_s[...] = jnp.transpose(hot)[:, :ROWS].astype(BF16)

    rate = jnp.transpose(decay_ref[...])
    weight = jnp.transpose(res_ref[...])
    twice = 2.0 * rate
    series = 1.0 - twice * (1.0 / 7.0)
    for term in (6.0, 5.0, 4.0, 3.0, 2.0):
        series = 1.0 - twice * (1.0 / term) * series
    scale = jnp.sqrt(twice * series)
    gain = weight * scale
    par_s[0] = rate
    par_s[1] = gain
    par_s[2] = scale
    par_s[3] = weight
    for k in range(NODES):
        e_s[k] = jnp.exp(-rate * float(nodes[k]))
        ep_s[k] = jnp.exp(-rate * float(span - nodes[k]))
    node_col = node_ref[...]
    own_filter = jnp.zeros((NODES, chans), F32)
    for m in range(MODES):
        rate_row, gain_row = par_s[0, m : m + 1, :], par_s[1, m : m + 1, :]
        wave = gain_row * jnp.exp(-rate_row * node_col)
        gt_s[m] = wave
        gr_s[m] = gain_row * jnp.exp(-rate_row * (float(span) - node_col))
        own_filter = own_filter + wave
    hn_stage[...] = own_filter.astype(BF16)
    hn_recv[me] = own_filter.astype(BF16)

    pl.semaphore_wait(barrier, (n - 1) + (near - 1) + (groups - 1))

    halo = to_ctx(halo_stage, halo_recv, edge_sem.at[0], edge_sem.at[1], ahead)
    halo.start()

    def send_filter(r, carry):
        d = lax.rem(me + r, n)
        to_ctx(hn_stage, hn_recv.at[me], hn_send.at[d], hn_sem.at[me], d).start()
        return carry

    lax.fori_loop(1, n, send_filter, 0)
    halo.wait()
    xs[6:8, :] = jnp.where(me > 0, halo_recv[...], 0.0)

    def features(r, carry):
        d = lax.rem(me + r, n)
        at = lanes(d)
        letter_s[...] = dot(hot_s[...], tbl_s[:, at])
        mixed, gated = [], []
        tap = [tap_s[i : i + 1, at] for i in range(9)]
        for c in range(span // ROWS):
            low = c * ROWS
            lag = [xs[8 + low - j : 8 + low - j + ROWS, at] for j in range(3)]
            stream = []
            for s in range(3):
                part = letter_s[s * span + low : s * span + low + ROWS, :]
                for j in range(3):
                    part = part + tap[3 * s + j] * lag[j]
                stream.append(part)
            key_s[low : low + ROWS, at] = stream[1]
            value_s[low : low + ROWS, at] = stream[2]
            mixed.append((stream[1] * stream[2]).astype(BF16))
            gated.append((cot_ref[low : low + ROWS, at].astype(F32) * stream[0]).astype(BF16))
        m_out = dot(fwd_ref[...], jnp.concatenate(mixed + mixed, axis=0))
        g_out = dot(fwd_ref[...], jnp.concatenate(gated + gated, axis=0))
        spec_m[:, at] = m_out[: 2 * span]
        spec_g[:, at] = g_out[: 2 * span]
        sums = jnp.concatenate([m_out[2 * span :], g_out[2 * span :]], axis=0).astype(BF16)
        pq_stage[d] = sums

        @pl.when(r < n)
        def _():
            to_ctx(pq_stage.at[d], pq_recv.at[me], pq_send.at[d], pq_sem.at[me], d).start()

        @pl.when(r == n)
        def _():
            pq_recv[me] = sums

        return carry

    lax.fori_loop(1, n + 1, features, 0)

    def take_filter(r, carry):
        d = lax.rem(me + r, n)
        to_ctx(hn_stage, hn_recv.at[d], hn_send.at[d], hn_sem.at[d], d).wait()
        return carry

    lax.fori_loop(1, n, take_filter, 0)

    def inside(r, carry):
        d = lax.rem(me + r, n)
        at = lanes(d)
        own = hn_recv[d]
        prod_s[...] = dot(resp_ref[...], jnp.concatenate([own, own], axis=0))
        conv_f, back_f, grad_f = [[], []], [[], []], [[], []]
        for c in range(span // ROWS):
            re, im = slice(c * ROWS, c * ROWS + ROWS), slice(span + c * ROWS, span + c * ROWS + ROWS)
            hr, hi = prod_s[re, :], prod_s[im, :]
            mr, mi = spec_m[re, at], spec_m[im, at]
            gr, gi = spec_g[re, at], spec_g[im, at]
            conv_f[0].append((hr * mr - hi * mi).astype(BF16))
            conv_f[1].append((hr * mi + hi * mr).astype(BF16))
            back_f[0].append((hr * gr + hi * gi).astype(BF16))
            back_f[1].append((hr * gi - hi * gr).astype(BF16))
            grad_f[0].append((gr * mr + gi * mi).astype(BF16))
            grad_f[1].append((gi * mr - gr * mi).astype(BF16))
        near_c[:, at] = dot(inv_ref[...], jnp.concatenate(conv_f[0] + conv_f[1], axis=0))
        near_b[:, at] = dot(inv_ref[...], jnp.concatenate(back_f[0] + back_f[1], axis=0))
        both = dot(gather_ref[...], jnp.concatenate(grad_f[0] + grad_f[1], axis=0))
        sums = both[:NODES] + both[NODES:]
        fgn_stage[d] = sums

        @pl.when(r < n)
        def _():
            to_ctx(fgn_stage.at[d], fgn_recv.at[me], fgn_send.at[d], fgn_sem.at[me], d).start()

        @pl.when(r == n)
        def _():
            fgn_recv[me] = sums

        return carry

    split_at = 1 + n // 2
    lax.fori_loop(1, split_at, inside, 0)

    def take_sums(r, carry):
        d = lax.rem(me + r, n)
        to_ctx(pq_stage.at[d], pq_recv.at[d], pq_send.at[d], pq_sem.at[d], d).wait()
        return carry

    lax.fori_loop(1, n, take_sums, 0)

    def states(j, carry):
        row_s[...] = pq_recv[j].astype(F32)
        a_sum = jnp.zeros((MODES, chans), F32)
        r_sum = jnp.zeros((MODES, chans), F32)
        for k in range(NODES):
            a_sum = a_sum + row_s[k : k + 1, :] * ep_s[k]
            r_sum = r_sum + row_s[NODES + k : NODES + k + 1, :] * e_s[k]
        a_s[j] = a_sum
        r_s[j] = r_sum
        return carry

    lax.fori_loop(0, n, states, 0)
    step = jnp.exp(-par_s[0] * float(span))

    def recur(i, carry):
        forward_state, backward_state = carry
        s_s[i] = forward_state
        u_s[n - 1 - i] = backward_state
        return step * forward_state + a_s[i], step * backward_state + r_s[n - 1 - i]

    nothing = jnp.zeros((MODES, chans), F32)
    lax.fori_loop(0, n, recur, (nothing, nothing))

    def respond(r, carry):
        d = lax.rem(me + r, n)
        y_sum = jnp.zeros((NODES, chans), F32)
        z_sum = jnp.zeros((NODES, chans), F32)
        for m in range(MODES):
            y_sum = y_sum + s_s[d, m : m + 1, :] * gt_s[m]
            z_sum = z_sum + u_s[d, m : m + 1, :] * gr_s[m]
        answer = jnp.concatenate([y_sum, z_sum], axis=0).astype(BF16)
        yz_stage[d] = answer

        @pl.when(r < n)
        def _():
            to_ctx(yz_stage.at[d], yz_recv.at[me], yz_send.at[d], yz_sem.at[me], d).start()

        @pl.when(r == n)
        def _():
            yz_recv[me] = answer

        return carry

    lax.fori_loop(1, n + 1, respond, 0)
    lax.fori_loop(split_at, n + 1, inside, 0)

    w_s[1, span : span + 8, :] = jnp.zeros((8, chans), F32)
    w_s[2, span : span + 8, :] = jnp.zeros((8, chans), F32)
    piece_stage[...] = jnp.zeros_like(piece_stage)

    def finish(r, carry):
        d = lax.rem(me + r, n)
        at = lanes(d)

        @pl.when(r < n)
        def _():
            to_ctx(yz_stage.at[d], yz_recv.at[d], yz_send.at[d], yz_sem.at[d], d).wait()

        y_node, z_node = yz_recv[d, :NODES], yz_recv[d, NODES:]
        far_s[0] = dot(spread_ref[...], jnp.concatenate([y_node, y_node], axis=0))
        far_s[1] = dot(spread_ref[...], jnp.concatenate([z_node, z_node], axis=0))
        tap = [tap_s[i : i + 1, at] for i in range(9)]
        totals = [jnp.zeros((8, chans), F32) for _ in range(9)]
        for c in range(span // ROWS):
            low = c * ROWS
            rows = slice(low, low + ROWS)
            conv = (near_c[rows, at] + far_s[0, rows, :]).astype(BF16).astype(F32)
            back = (near_b[rows, at] + far_s[1, rows, :]).astype(BF16).astype(F32)
            grads = [
                cot_ref[rows, at].astype(F32) * conv,
                back * value_s[rows, at],
                back * key_s[rows, at],
            ]
            lag = [xs[8 + low - j : 8 + low - j + ROWS, at] for j in range(3)]
            for s in range(3):
                fg_s[s * span + low : s * span + low + ROWS, :] = grads[s].astype(BF16)
                for j in range(3):
                    part = grads[s] * lag[j]
                    totals[3 * s + j] = totals[3 * s + j] + (part[:8] + part[8:])
            for j in range(3):
                w_s[j, rows, :] = tap[j] * grads[0] + tap[3 + j] * grads[1] + tap[6 + j] * grads[2]
        piece_stage[d, :ROWS, :] = dot(hot_t[...], fg_s[...])
        for i in range(9):
            piece_stage[d, 12 + i : 13 + i, :] = jnp.sum(totals[i], axis=0, keepdims=True)
        for c in range(span // ROWS):
            low = c * ROWS
            part = (
                w_s[0, low : low + ROWS, :]
                + w_s[1, low + 1 : low + 1 + ROWS, :]
                + w_s[2, low + 2 : low + 2 + ROWS, :]
            )
            if c < span // ROWS - 1:
                grad_ref[low : low + ROWS, at] = part.astype(BF16)
            else:
                tail_s[:, at] = part
        edge_stage[0:1, at] = w_s[2, 0:1, :]
        edge_stage[1:2, at] = w_s[1, 0:1, :] + w_s[2, 1:2, :]

        @pl.when(r < n)
        def _():
            to_ctx(piece_stage.at[d], piece_recv.at[me], piece_send.at[d], piece_sem.at[me], d).start()

        @pl.when(r == n)
        def _():
            piece_recv[me] = piece_stage[d]

        return carry

    lax.fori_loop(1, n + 1, finish, 0)
    edge = to_ctx(edge_stage, edge_recv, edge_sem.at[2], edge_sem.at[3], behind)
    edge.start()

    def lags(j, carry):
        sums = pq_recv[j].astype(F32)
        row_s[:NODES] = sums[:NODES] * (float(span) - node_col)
        row_s[NODES:] = sums[NODES:] * node_col
        a_sum = jnp.zeros((MODES, chans), F32)
        r_sum = jnp.zeros((MODES, chans), F32)
        for k in range(NODES):
            a_sum = a_sum + row_s[k : k + 1, :] * ep_s[k]
            r_sum = r_sum + row_s[NODES + k : NODES + k + 1, :] * e_s[k]
        al_s[j] = a_sum
        rl_s[j] = r_sum
        return carry

    lax.fori_loop(0, n, lags, 0)

    def pair(i, carry):
        lag_state, exp_sum, lag_sum = carry
        state, reach = s_s[i], r_s[i]
        exp_sum = exp_sum + reach * state
        lag_sum = lag_sum + rl_s[i] * state + reach * lag_state
        return step * (lag_state + float(span) * state) + al_s[i], exp_sum, lag_sum

    _, exp_sum, lag_sum = lax.fori_loop(0, n, pair, (nothing, nothing, nothing))

    def take_near(r, carry):
        d = lax.rem(me + r, n)
        to_ctx(fgn_stage.at[d], fgn_recv.at[d], fgn_send.at[d], fgn_sem.at[d], d).wait()
        return carry

    lax.fori_loop(1, n, take_near, 0)
    near_sum = fgn_recv[0]
    for d in range(1, n):
        near_sum = near_sum + fgn_recv[d]
    row_s[:NODES] = near_sum
    row_s[NODES:] = near_sum * node_col
    for k in range(NODES):
        exp_sum = exp_sum + row_s[k : k + 1, :] * e_s[k]
        lag_sum = lag_sum + row_s[NODES + k : NODES + k + 1, :] * e_s[k]
    scale, weight = par_s[2], par_s[3]
    pay[PIECE : PIECE + MODES, :] = scale * exp_sum
    pay[PIECE + MODES : PIECE + 2 * MODES, :] = (
        weight * jnp.exp(-2.0 * par_s[0]) / scale * exp_sum - par_s[1] * lag_sum
    )
    pay[PIECE + 2 * MODES :, :] = jnp.zeros((PAY - PIECE - 2 * MODES, chans), F32)

    def take_piece(r, carry):
        d = lax.rem(me + r, n)
        to_ctx(piece_stage.at[d], piece_recv.at[d], piece_send.at[d], piece_sem.at[d], d).wait()
        return carry

    lax.fori_loop(1, n, take_piece, 0)
    piece = piece_recv[0]
    for d in range(1, n):
        piece = piece + piece_recv[d]
    pay[:PIECE, :] = piece

    def part_of(p):
        return pay.at[pl.ds(pl.multiple_of(p * chunk, 8), chunk), :]

    def scatter(r, carry):
        p = lax.rem(mine + r, near)
        to_dp(part_of(p), one_recv.at[mine], one_send.at[p], one_sem.at[mine], block * near + p).start()
        return carry

    lax.fori_loop(1, near, scatter, 0)
    one_recv[mine] = part_of(mine)[...]

    edge.wait()
    tail_s[ROWS - 2 :, :] = tail_s[ROWS - 2 :, :] + jnp.where(me < n - 1, edge_recv[...], 0.0)
    grad_ref[span - ROWS :, :] = tail_s[...].astype(BF16)

    def take_one(r, carry):
        p = lax.rem(mine + r, near)
        to_dp(part_of(p), one_recv.at[p], one_send.at[p], one_sem.at[p], block * near + p).wait()
        return carry

    lax.fori_loop(1, near, take_one, 0)
    total = one_recv[0]
    for p in range(1, near):
        total = total + one_recv[p]
    two_recv[block] = total

    def swap(r, carry):
        b = lax.rem(block + r, groups)
        to_dp(two_recv.at[block], two_recv.at[block], two_send.at[b], two_sem.at[block], b * near + mine).start()
        return carry

    def take_two(r, carry):
        b = lax.rem(block + r, groups)
        to_dp(two_recv.at[b], two_recv.at[b], two_send.at[b], two_sem.at[b], b * near + mine).wait()
        return carry

    lax.fori_loop(1, groups, swap, 0)
    lax.fori_loop(1, groups, take_two, 0)
    total = two_recv[0]
    for b in range(1, groups):
        total = total + two_recv[b]
    three_recv[mine] = total

    def share(r, carry):
        p = lax.rem(mine + r, near)
        to_dp(three_recv.at[mine], three_recv.at[mine], three_send.at[p], three_sem.at[mine], block * near + p).start()
        return carry

    def take_three(r, carry):
        p = lax.rem(mine + r, near)
        to_dp(three_recv.at[p], three_recv.at[p], three_send.at[p], three_sem.at[p], block * near + p).wait()
        return carry

    lax.fori_loop(1, near, share, 0)
    lax.fori_loop(1, near, take_three, 0)
    result = jnp.concatenate([three_recv[p] for p in range(near)], axis=0)
    for s in range(3):
        table_out[s] = result[4 * s : 4 * s + 4]
        taps_out[s] = result[12 + 3 * s : 15 + 3 * s]
    res_out[...] = jnp.transpose(result[PIECE : PIECE + MODES])
    decay_out[...] = jnp.transpose(result[PIECE + MODES : PIECE + 2 * MODES])


def shards(n, near, groups, inputs, letters, letter_table, short_taps, residues, decay_rate, cotangent):
    span, width = inputs.shape[1:]
    chans = width // n
    fixed = tables(span)
    nodes = fixed["nodes"]
    node_cols = jnp.asarray(np.broadcast_to(nodes[:, None], (NODES, chans)).astype(np.float32))
    vmem = pl.BlockSpec(memory_space=pltpu.VMEM)
    dma = pltpu.SemaphoreType.DMA
    scratch = [
        pltpu.VMEM((span + 8, width), F32),
        pltpu.VMEM((span, width), F32),
        pltpu.VMEM((span, width), F32),
        pltpu.VMEM((2 * span, width), F32),
        pltpu.VMEM((2 * span, width), F32),
        pltpu.VMEM((span, width), F32),
        pltpu.VMEM((span, width), F32),
        pltpu.VMEM((3 * span, chans), F32),
        pltpu.VMEM((3 * span, ROWS), BF16),
        pltpu.VMEM((ROWS, 3 * span), BF16),
        pltpu.VMEM((ROWS, width), BF16),
        pltpu.VMEM((ROWS, width), F32),
        pltpu.VMEM((2 * span, chans), F32),
        pltpu.VMEM((2, span, chans), F32),
        pltpu.VMEM((3 * span, chans), BF16),
        pltpu.VMEM((3, span + 8, chans), F32),
        pltpu.VMEM((ROWS, width), F32),
        pltpu.VMEM((NODES, MODES, chans), F32),
        pltpu.VMEM((NODES, MODES, chans), F32),
        pltpu.VMEM((MODES, NODES, chans), F32),
        pltpu.VMEM((MODES, NODES, chans), F32),
        pltpu.VMEM((n, MODES, chans), F32),
        pltpu.VMEM((n, MODES, chans), F32),
        pltpu.VMEM((n, MODES, chans), F32),
        pltpu.VMEM((n, MODES, chans), F32),
        pltpu.VMEM((n, MODES, chans), F32),
        pltpu.VMEM((n, MODES, chans), F32),
        pltpu.VMEM((2 * NODES, chans), F32),
        pltpu.VMEM((4, MODES, chans), F32),
        pltpu.VMEM((2, width), F32),
        pltpu.VMEM((2, width), F32),
        pltpu.VMEM((2, width), F32),
        pltpu.VMEM((2, width), F32),
        pltpu.VMEM((NODES, chans), BF16),
        pltpu.VMEM((n, NODES, chans), BF16),
        pltpu.VMEM((n, 2 * NODES, chans), BF16),
        pltpu.VMEM((n, 2 * NODES, chans), BF16),
        pltpu.VMEM((n, NODES, chans), F32),
        pltpu.VMEM((n, NODES, chans), F32),
        pltpu.VMEM((n, 2 * NODES, chans), BF16),
        pltpu.VMEM((n, 2 * NODES, chans), BF16),
        pltpu.VMEM((n, PIECE, chans), F32),
        pltpu.VMEM((n, PIECE, chans), F32),
        pltpu.VMEM((PAY, chans), F32),
        pltpu.VMEM((near, PAY // near, chans), F32),
        pltpu.VMEM((groups, PAY // near, chans), F32),
        pltpu.VMEM((near, PAY // near, chans), F32),
        dma((4,)),
    ] + [dma((n,))] * 10 + [dma((near,))] * 2 + [dma((groups,))] * 2 + [dma((near,))] * 2
    grad, taps_grad, table_grad, residue_grad, decay_grad = pl.pallas_call(
        functools.partial(kernel, n, near, groups, span, chans, nodes),
        out_shape=(
            jax.ShapeDtypeStruct((span, width), BF16),
            jax.ShapeDtypeStruct((3, 3, chans), F32),
            jax.ShapeDtypeStruct((3, 4, chans), F32),
            jax.ShapeDtypeStruct((chans, MODES), F32),
            jax.ShapeDtypeStruct((chans, MODES), F32),
        ),
        in_specs=[vmem] * 13,
        out_specs=(vmem,) * 5,
        scratch_shapes=scratch,
        compiler_params=pltpu.CompilerParams(
            collective_id=0, has_side_effects=True, vmem_limit_bytes=48 * 1024 * 1024
        ),
    )(
        inputs[0],
        letters,
        letter_table,
        short_taps,
        residues,
        decay_rate,
        cotangent[0],
        jnp.asarray(fixed["forward"]),
        jnp.asarray(fixed["inverse"]),
        jnp.asarray(fixed["spread"]),
        jnp.asarray(fixed["response"]),
        jnp.asarray(fixed["gather"]),
        node_cols,
    )
    return grad[None], taps_grad, table_grad, residue_grad, decay_grad


def solution(mesh):
    n, sequences = mesh.shape["ctx"], mesh.shape["dp"]
    near = max(k for k in (1, 2, 4, 8) if sequences % k == 0 and k * k <= 2 * sequences)
    in_specs = (
        P("dp", "ctx", None),
        P("dp", "ctx"),
        P(),
        P(),
        P("ctx", None),
        P("ctx", None),
        P("dp", "ctx", None),
    )
    out_specs = (
        P("dp", "ctx", None),
        P(None, None, "ctx"),
        P(None, None, "ctx"),
        P("ctx", None),
        P("ctx", None),
    )
    body = functools.partial(shards, n, near, sequences // near)
    return jax.shard_map(body, mesh=mesh, in_specs=in_specs, out_specs=out_specs, check_vma=False)
```

```python
import functools

import jax
import jax.numpy as jnp
import numpy as np
from jax import lax
from jax.experimental import pallas as pl
from jax.experimental.pallas import tpu as pltpu
from jax.sharding import PartitionSpec as P

MESH = pl.DeviceIdType.MESH
F32 = jnp.float32
BF16 = jnp.bfloat16
NODES = 16
MODES = 16
ROWS = 16
PIECE = 24
GRADS = 2 * MODES
LANES = 128


def split(values):
    high = values.astype(jnp.bfloat16)
    low = (values - high.astype(np.float64)).astype(jnp.bfloat16)
    return high, low


def tables(span):
    half = span / 2
    centre = (span - 1) / 2
    angles = np.pi * (2 * np.arange(NODES) + 1) / (2 * NODES)
    nodes = centre + half * np.cos(angles)
    places = np.arange(span)
    interp = np.ones((span, NODES))
    for k in range(NODES):
        for other in range(NODES):
            if other != k:
                interp[:, k] *= (places - nodes[other]) / (nodes[k] - nodes[other])
    theta = 2 * np.pi * (np.arange(span) + 0.5) / (2 * span)
    phase = theta[:, None] * places[None, :]
    forward = np.concatenate([np.cos(phase), -np.sin(phase)], axis=0)
    inverse = np.concatenate([np.cos(phase.T), -np.sin(phase.T)], axis=1) / span
    l_hi, l_lo = split(interp)
    w_hi, w_lo = split(forward @ interp)
    m_hi, m_lo = split(interp.T @ inverse)
    return dict(
        nodes=nodes,
        forward=forward.astype(jnp.bfloat16),
        moments=np.concatenate([l_hi.T, l_lo.T], axis=0),
        inverse=np.concatenate([inverse, m_hi.astype(np.float64), m_lo.astype(np.float64)], axis=0).astype(np.float32),
        spread=np.concatenate([l_hi, l_lo], axis=1),
        response=np.concatenate([w_hi, w_lo], axis=1),
    )


def dot(left, right):
    return jnp.dot(left, right, preferred_element_type=F32)


def kernel(n, near, groups, wide, span, chans, nodes, *refs):
    (
        x_hbm, letters_hbm, table_hbm, taps_hbm, res_hbm, decay_hbm, cot_hbm,
        fwd_hbm, mom_hbm, inv_hbm, spread_hbm, resp_hbm, node_hbm,
        grad_hbm, total_ref,
        x_ref, letters_ref, table_ref, taps_ref, res_ref, decay_ref, cot_ref,
        fwd_ref, mom_ref, inv_ref, spread_ref, resp_ref, node_ref,
        x_last, inv_s, grad_ref, xs, key_s, value_s, mix_s, gate_s, conv_s, back_s,
        code_s, hot_t, tab_s, tap_s, spec_m, spec_g, spec_h, prod_s, far_s, fg_s, w_s, tail_s,
        e_s, ep_s, gt_s, gr_s, a_s, r_s, s_s, u_s, al_s, rl_s, row_s, par_s,
        halo_stage, halo_recv, edge_stage, edge_recv,
        hn_stage, hn_recv, pq_stage, pq_recv, fgn_stage, fgn_recv,
        yz_stage, yz_recv, piece_stage, piece_recv,
        mode_stage, mode_one, mode_two, mode_three, tap_near, tap_far,
        in_sem, out_sem, edge_sem,
        hn_send, hn_sem, pq_send, pq_sem, fgn_send, fgn_sem, yz_send, yz_sem, piece_send, piece_sem,
        mo_send, mo_sem, mt_send, mt_sem, mh_send, mh_sem, tn_send, tn_sem, tf_send, tf_sem,
    ) = refs
    me = lax.axis_index("ctx")
    seq = lax.axis_index("dp")
    mine, block = lax.rem(seq, near), seq // near
    ahead, behind = lax.rem(me + 1, n), lax.rem(me + n - 1, n)
    sets = n // wide
    width = wide * chans
    chunks = span // ROWS

    def lanes(d):
        return pl.ds(pl.multiple_of(d * chans, chans), chans)

    def set_lanes(first):
        return pl.ds(pl.multiple_of(first * chans, width), width)

    def first_of(r):
        return lax.rem(me // wide + r, sets) * wide

    def to_ctx(source, target, send, recv, d):
        return pltpu.make_async_remote_copy(
            src_ref=source, dst_ref=target, send_sem=send, recv_sem=recv,
            device_id=(seq, d), device_id_type=MESH,
        )

    def to_dp(source, target, send, recv, p):
        return pltpu.make_async_remote_copy(
            src_ref=source, dst_ref=target, send_sem=send, recv_sem=recv,
            device_id=(p, me), device_id_type=MESH,
        )

    def send_others(first, stage, recv_buffer, send, recv):
        for g in range(wide):
            d = first + g

            @pl.when(d != me)
            def _():
                to_ctx(stage.at[d], recv_buffer.at[me], send.at[d], recv.at[me], d).start()

    def take_others(stage, recv_buffer, send, recv):
        def take(r, carry):
            d = lax.rem(me + r, n)
            to_ctx(stage.at[d], recv_buffer.at[d], send.at[d], recv.at[d], d).wait()
            return carry

        lax.fori_loop(1, n, take, 0)

    barrier = pltpu.get_barrier_semaphore()

    def greet_ctx(r, carry):
        pl.semaphore_signal(barrier, inc=1, device_id=(seq, lax.rem(me + r, n)), device_id_type=MESH)
        return carry

    def greet_near(r, carry):
        peer = block * near + lax.rem(mine + r, near)
        pl.semaphore_signal(barrier, inc=1, device_id=(peer, me), device_id_type=MESH)
        return carry

    def greet_far(r, carry):
        peer = lax.rem(block + r, groups) * near + mine
        pl.semaphore_signal(barrier, inc=1, device_id=(peer, me), device_id_type=MESH)
        return carry

    lax.fori_loop(1, n, greet_ctx, 0)
    lax.fori_loop(1, near, greet_near, 0)
    lax.fori_loop(1, groups, greet_far, 0)

    loads = [
        pltpu.make_async_copy(source, target, in_sem.at[i])
        for i, (source, target) in enumerate([
            (x_hbm.at[pl.ds(span - ROWS, ROWS), :], x_last), (x_hbm, x_ref),
            (letters_hbm, letters_ref), (table_hbm, table_ref), (taps_hbm, taps_ref), (cot_hbm, cot_ref),
            (mom_hbm, mom_ref), (res_hbm, res_ref), (decay_hbm, decay_ref), (node_hbm, node_ref),
            (fwd_hbm, fwd_ref), (inv_hbm, inv_ref), (resp_hbm, resp_ref), (spread_hbm, spread_ref),
        ])
    ]
    for load in loads:
        load.start()
    loads[0].wait()
    halo_stage[...] = x_last[...].astype(F32)[ROWS - 2 :, :]
    pl.semaphore_wait(barrier, (n - 1) + (near - 1) + (groups - 1))
    halo = to_ctx(halo_stage, halo_recv, edge_sem.at[0], edge_sem.at[1], ahead)
    halo.start()
    for load in loads[1:6]:
        load.wait()

    codes = jnp.concatenate([letters_ref[...] + 4 * s for s in range(3)], axis=1)
    hot_t[...] = (lax.broadcasted_iota(jnp.int32, (ROWS, 3 * span), 0) == codes).astype(F32).astype(BF16)
    code_s[...] = jnp.transpose(jnp.broadcast_to(letters_ref[...].astype(F32), (LANES, span)))

    def products(at, which):
        tap = [tap_s[i : i + 1, at] for i in range(9)]
        tab = [tab_s[i : i + 1, at] for i in range(12)]
        for c in which:
            low = c * ROWS
            rows = slice(low, low + ROWS)
            code = code_s[rows, :]
            is_one, is_two, is_three = code == 1.0, code == 2.0, code == 3.0
            lag = [xs[8 + low - j : 8 + low - j + ROWS, at] for j in range(3)]
            stream = []
            for s in range(3):
                part = jnp.where(
                    is_one,
                    tab[4 * s + 1],
                    jnp.where(is_two, tab[4 * s + 2], jnp.where(is_three, tab[4 * s + 3], tab[4 * s])),
                )
                for j in range(3):
                    part = part + tap[3 * s + j] * lag[j]
                stream.append(part)
            key_s[rows, at] = stream[1]
            value_s[rows, at] = stream[2]
            mix_s[rows, at] = (stream[1] * stream[2]).astype(BF16)
            gate_s[rows, at] = (cot_ref[rows, at].astype(F32) * stream[0]).astype(BF16)

    def late_rows(g, carry):
        at = lanes(g)
        xs[8:, at] = x_ref[:, at].astype(F32)
        for s in range(3):
            tap_s[3 * s : 3 * s + 3, at] = taps_ref[s, :, at].astype(F32)
            tab_s[4 * s : 4 * s + 4, at] = table_ref[s, :, at].astype(F32)
        for t in range(chans // LANES):
            products(pl.ds(pl.multiple_of(g * chans + t * LANES, LANES), LANES), range(1, chunks))
        return carry

    lax.fori_loop(0, n, late_rows, 0)
    loads[6].wait()
    halo.wait()
    xs[6:8, :] = jnp.where(me > 0, halo_recv[...], 0.0)

    def node_sums(r, carry):
        first = first_of(r)
        for t in range(width // LANES):
            products(pl.ds(pl.multiple_of(first * chans + t * LANES, LANES), LANES), range(1))
        at = set_lanes(first)
        p_sum = dot(mom_ref[...], mix_s[:, at])
        q_sum = dot(mom_ref[...], gate_s[:, at])
        sums = jnp.concatenate([p_sum[:NODES] + p_sum[NODES:], q_sum[:NODES] + q_sum[NODES:]], axis=0).astype(BF16)
        for g in range(wide):
            pq_stage[first + g] = sums[:, g * chans : (g + 1) * chans]
        send_others(first, pq_stage, pq_recv, pq_send, pq_sem)
        return carry

    lax.fori_loop(1, sets + 1, node_sums, 0)
    pq_recv[me] = pq_stage[me]

    for load in loads[7:]:
        load.wait()
    rate, weight = decay_ref[...], res_ref[...]
    twice = 2.0 * rate
    series = 1.0 - twice * (1.0 / 7.0)
    for term in (6.0, 5.0, 4.0, 3.0, 2.0):
        series = 1.0 - twice * (1.0 / term) * series
    scale = jnp.sqrt(twice * series)
    gain = weight * scale
    par_s[0] = gain
    par_s[1] = scale
    node_col = node_ref[...]
    own_filter = jnp.zeros((NODES, chans), F32)
    for m in range(MODES):
        wave = par_s[0, m : m + 1, :] * jnp.exp(-decay_ref[m : m + 1, :] * node_col)
        gt_s[m] = wave
        own_filter = own_filter + wave
    hn_stage[...] = own_filter.astype(BF16)
    hn_recv[me] = own_filter.astype(BF16)

    def send_filter(r, carry):
        d = lax.rem(me + r, n)
        to_ctx(hn_stage, hn_recv.at[me], hn_send.at[d], hn_sem.at[me], d).start()
        return carry

    lax.fori_loop(1, n, send_filter, 0)
    for m in range(MODES):
        gr_s[m] = par_s[0, m : m + 1, :] * jnp.exp(-decay_ref[m : m + 1, :] * (float(span) - node_col))
    for k in range(NODES):
        e_s[k] = jnp.exp(-rate * float(nodes[k]))
        ep_s[k] = jnp.exp(-rate * float(span - nodes[k]))
    inv_s[...] = inv_ref[...].astype(BF16)

    def spectra(r, carry):
        first = first_of(r)
        at = set_lanes(first)
        spec_m[:, at] = dot(fwd_ref[...], mix_s[:, at])
        spec_g[:, at] = dot(fwd_ref[...], gate_s[:, at])

        def multiply(t, carry):
            some = pl.ds(pl.multiple_of(t * LANES, LANES), LANES)
            here = pl.ds(pl.multiple_of(first * chans + t * LANES, LANES), LANES)
            for c in range(chunks):
                re, im = slice(c * ROWS, c * ROWS + ROWS), slice(span + c * ROWS, span + c * ROWS + ROWS)
                mr, mi = spec_m[re, here], spec_m[im, here]
                gr, gi = spec_g[re, here], spec_g[im, here]
                prod_s[0, re, some] = (gr * mr + gi * mi).astype(BF16)
                prod_s[0, im, some] = (gi * mr - gr * mi).astype(BF16)
            return carry

        lax.fori_loop(0, width // LANES, multiply, 0)
        both = dot(inv_s[span:, :], prod_s[0])
        sums = both[:NODES] + both[NODES:]
        for g in range(wide):
            fgn_stage[first + g] = sums[:, g * chans : (g + 1) * chans]
        send_others(first, fgn_stage, fgn_recv, fgn_send, fgn_sem)
        return carry

    lax.fori_loop(1, sets + 1, spectra, 0)

    take_others(pq_stage, pq_recv, pq_send, pq_sem)

    def states(j, carry):
        row_s[...] = pq_recv[j].astype(F32)
        a_sum = jnp.zeros((MODES, chans), F32)
        r_sum = jnp.zeros((MODES, chans), F32)
        for k in range(NODES):
            a_sum = a_sum + row_s[k : k + 1, :] * ep_s[k]
            r_sum = r_sum + row_s[NODES + k : NODES + k + 1, :] * e_s[k]
        a_s[j] = a_sum
        r_s[j] = r_sum
        return carry

    lax.fori_loop(0, n, states, 0)
    step = jnp.exp(-decay_ref[...] * float(span))

    def recur(i, carry):
        forward_state, backward_state = carry
        s_s[i] = forward_state
        u_s[n - 1 - i] = backward_state
        return step * forward_state + a_s[i], step * backward_state + r_s[n - 1 - i]

    nothing = jnp.zeros((MODES, chans), F32)
    lax.fori_loop(0, n, recur, (nothing, nothing))

    def respond(r, carry):
        d = lax.rem(me + r, n)
        y_sum = jnp.zeros((NODES, chans), F32)
        z_sum = jnp.zeros((NODES, chans), F32)
        for m in range(MODES):
            y_sum = y_sum + s_s[d, m : m + 1, :] * gt_s[m]
            z_sum = z_sum + u_s[d, m : m + 1, :] * gr_s[m]
        yz_stage[d] = jnp.concatenate([y_sum, z_sum], axis=0).astype(BF16)

        @pl.when(r < n)
        def _():
            to_ctx(yz_stage.at[d], yz_recv.at[me], yz_send.at[d], yz_sem.at[me], d).start()

        return carry

    lax.fori_loop(1, n + 1, respond, 0)
    yz_recv[me] = yz_stage[me]

    def take_filter(r, carry):
        d = lax.rem(me + r, n)
        to_ctx(hn_stage, hn_recv.at[d], hn_send.at[d], hn_sem.at[d], d).wait()
        return carry

    lax.fori_loop(1, n, take_filter, 0)

    def inside(r, carry):
        first = first_of(r)
        at = set_lanes(first)
        own = jnp.concatenate([hn_recv[first + g] for g in range(wide)], axis=1)
        spec_h[...] = dot(resp_ref[...], jnp.concatenate([own, own], axis=0))

        def multiply(t, carry):
            some = pl.ds(pl.multiple_of(t * LANES, LANES), LANES)
            here = pl.ds(pl.multiple_of(first * chans + t * LANES, LANES), LANES)
            for c in range(chunks):
                re, im = slice(c * ROWS, c * ROWS + ROWS), slice(span + c * ROWS, span + c * ROWS + ROWS)
                hr, hi = spec_h[re, some], spec_h[im, some]
                mr, mi = spec_m[re, here], spec_m[im, here]
                gr, gi = spec_g[re, here], spec_g[im, here]
                prod_s[0, re, some] = (hr * mr - hi * mi).astype(BF16)
                prod_s[0, im, some] = (hr * mi + hi * mr).astype(BF16)
                prod_s[1, re, some] = (hr * gr + hi * gi).astype(BF16)
                prod_s[1, im, some] = (hr * gi - hi * gr).astype(BF16)
            return carry

        lax.fori_loop(0, width // LANES, multiply, 0)
        conv_s[:, at] = dot(inv_s[:span, :], prod_s[0])
        back_s[:, at] = dot(inv_s[:span, :], prod_s[1])
        return carry

    lax.fori_loop(1, sets + 1, inside, 0)

    def lags(j, carry):
        sums = pq_recv[j].astype(F32)
        row_s[:NODES] = sums[:NODES] * (float(span) - node_ref[...])
        row_s[NODES:] = sums[NODES:] * node_ref[...]
        a_sum = jnp.zeros((MODES, chans), F32)
        r_sum = jnp.zeros((MODES, chans), F32)
        for k in range(NODES):
            a_sum = a_sum + row_s[k : k + 1, :] * ep_s[k]
            r_sum = r_sum + row_s[NODES + k : NODES + k + 1, :] * e_s[k]
        al_s[j] = a_sum
        rl_s[j] = r_sum
        return carry

    lax.fori_loop(0, n, lags, 0)

    def pair(i, carry):
        lag_state, exp_sum, lag_sum = carry
        state, reach = s_s[i], r_s[i]
        exp_sum = exp_sum + reach * state
        lag_sum = lag_sum + rl_s[i] * state + reach * lag_state
        return step * (lag_state + float(span) * state) + al_s[i], exp_sum, lag_sum

    _, exp_sum, lag_sum = lax.fori_loop(0, n, pair, (nothing, nothing, nothing))
    take_others(fgn_stage, fgn_recv, fgn_send, fgn_sem)
    fgn_recv[me] = fgn_stage[me]
    near_sum = fgn_recv[0]
    for d in range(1, n):
        near_sum = near_sum + fgn_recv[d]
    row_s[:NODES] = near_sum
    row_s[NODES:] = near_sum * node_ref[...]
    for k in range(NODES):
        exp_sum = exp_sum + row_s[k : k + 1, :] * e_s[k]
        lag_sum = lag_sum + row_s[NODES + k : NODES + k + 1, :] * e_s[k]
    mode_grads = (
        par_s[1] * exp_sum,
        res_ref[...] * jnp.exp(-2.0 * decay_ref[...]) / par_s[1] * exp_sum - par_s[0] * lag_sum,
    )

    def tile_of(index):
        row, lane = index // (chans // LANES), index % (chans // LANES)
        per = GRADS // 8 * (chans // LANES) // near
        return row // 2, row % 2 * 8, lane * LANES, index // per, index % per * 8

    tiles = range(GRADS // 8 * (chans // LANES))
    for index in tiles:
        which, row, lane, slot, place = tile_of(index)
        mode_stage[slot, place : place + 8, :] = mode_grads[which][row : row + 8, lane : lane + LANES]

    def send_near(source, target, send, recv):
        def one(r, carry):
            p = lax.rem(mine + r, near)
            to_dp(source(p), target.at[mine], send.at[p], recv.at[mine], block * near + p).start()
            return carry

        lax.fori_loop(1, near, one, 0)

    def take_near(target, send, recv):
        def one(r, carry):
            p = lax.rem(mine + r, near)
            to_dp(target.at[p], target.at[p], send.at[p], recv.at[p], block * near + p).wait()
            return carry

        lax.fori_loop(1, near, one, 0)

    def send_far(target, send, recv):
        def one(r, carry):
            b = lax.rem(block + r, groups)
            to_dp(target.at[block], target.at[block], send.at[b], recv.at[block], b * near + mine).start()
            return carry

        lax.fori_loop(1, groups, one, 0)

    def take_far(target, send, recv):
        def one(r, carry):
            b = lax.rem(block + r, groups)
            to_dp(target.at[b], target.at[b], send.at[b], recv.at[b], b * near + mine).wait()
            return carry

        lax.fori_loop(1, groups, one, 0)

    def sum_of(buffer):
        total = buffer[0]
        for p in range(1, buffer.shape[0]):
            total = total + buffer[p]
        return total

    send_near(lambda p: mode_stage.at[p], mode_one, mo_send, mo_sem)
    mode_one[mine] = mode_stage[mine]

    def finish(r, carry):
        first = first_of(r)
        for g in range(wide):
            d = first + g

            @pl.when(d != me)
            def _():
                to_ctx(yz_stage.at[d], yz_recv.at[d], yz_send.at[d], yz_sem.at[d], d).wait()

        y_node = jnp.concatenate([yz_recv[first + g, :NODES] for g in range(wide)], axis=1)
        z_node = jnp.concatenate([yz_recv[first + g, NODES:] for g in range(wide)], axis=1)
        far_s[0] = dot(spread_ref[...], jnp.concatenate([y_node, y_node], axis=0))
        far_s[1] = dot(spread_ref[...], jnp.concatenate([z_node, z_node], axis=0))

        def gradients(g, carry):
            for t in range(chans // LANES):
                some = pl.ds(pl.multiple_of(g * chans + t * LANES, LANES), LANES)
                at = pl.ds(pl.multiple_of((first + g) * chans + t * LANES, LANES), LANES)
                totals = [jnp.zeros((8, LANES), F32) for _ in range(9)]
                for c in range(chunks):
                    low = c * ROWS
                    rows = slice(low, low + ROWS)
                    conv = (conv_s[rows, at] + far_s[0, rows, some]).astype(BF16).astype(F32)
                    back = (back_s[rows, at] + far_s[1, rows, some]).astype(BF16).astype(F32)
                    conv_s[rows, at] = conv
                    back_s[rows, at] = back
                    grads = [
                        cot_ref[rows, at].astype(F32) * conv,
                        back * value_s[rows, at],
                        back * key_s[rows, at],
                    ]
                    lag = [xs[8 + low - j : 8 + low - j + ROWS, at] for j in range(3)]
                    for s in range(3):
                        fg_s[s * span + low : s * span + low + ROWS, some] = grads[s].astype(BF16)
                        for j in range(3):
                            part = grads[s] * lag[j]
                            totals[3 * s + j] = totals[3 * s + j] + (part[:8] + part[8:])
                for i in range(9):
                    piece_stage[first + g, 12 + i : 13 + i, t * LANES : (t + 1) * LANES] = jnp.sum(
                        totals[i], axis=0, keepdims=True
                    )
            return carry

        lax.fori_loop(0, wide, gradients, 0)
        letter_sums = dot(hot_t[...], fg_s[...])
        for g in range(wide):
            piece_stage[first + g, :12, :] = letter_sums[:12, g * chans : (g + 1) * chans]
            piece_stage[first + g, 21:, :] = jnp.zeros((PIECE - 21, chans), F32)
        send_others(first, piece_stage, piece_recv, piece_send, piece_sem)
        return carry

    lax.fori_loop(1, sets + 1, finish, 0)

    take_near(mode_one, mo_send, mo_sem)
    mode_two[block] = sum_of(mode_one)
    send_far(mode_two, mt_send, mt_sem)

    take_others(piece_stage, piece_recv, piece_send, piece_sem)
    piece_recv[me] = piece_stage[me]
    tap_near[mine] = sum_of(piece_recv)
    send_near(lambda p: tap_near.at[mine], tap_near, tn_send, tn_sem)

    w_s[0, span : span + 8, :] = jnp.zeros((8, chans), F32)
    w_s[1, span : span + 8, :] = jnp.zeros((8, chans), F32)

    def input_gradient(d, carry):
        for t in range(chans // LANES):
            some = slice(t * LANES, (t + 1) * LANES)
            at = pl.ds(pl.multiple_of(d * chans + t * LANES, LANES), LANES)
            tap = [tap_s[i : i + 1, at] for i in range(9)]
            for c in reversed(range(chunks)):
                low = c * ROWS
                rows = slice(low, low + ROWS)
                back = back_s[rows, at]
                grads = [cot_ref[rows, at].astype(F32) * conv_s[rows, at], back * value_s[rows, at], back * key_s[rows, at]]
                ahead_by = [tap[j] * grads[0] + tap[3 + j] * grads[1] + tap[6 + j] * grads[2] for j in range(3)]
                w_s[0, rows, some] = ahead_by[1]
                w_s[1, rows, some] = ahead_by[2]
                part = (
                    ahead_by[0]
                    + w_s[0, low + 1 : low + 1 + ROWS, some]
                    + w_s[1, low + 2 : low + 2 + ROWS, some]
                )
                if c < chunks - 1:
                    grad_ref[rows, at] = part.astype(BF16)
                else:
                    tail_s[:, at] = part
            edge_stage[0:1, at] = w_s[1, 0:1, some]
            edge_stage[1:2, at] = w_s[0, 0:1, some] + w_s[1, 1:2, some]
        return carry

    lax.fori_loop(0, n, input_gradient, 0)
    edge = to_ctx(edge_stage, edge_recv, edge_sem.at[2], edge_sem.at[3], behind)
    edge.start()
    body = pl.ds(0, span - ROWS)
    main = pltpu.make_async_copy(grad_ref.at[body, :], grad_hbm.at[body, :], out_sem.at[0])
    main.start()

    take_near(tap_near, tn_send, tn_sem)
    tap_far[block] = sum_of(tap_near)
    send_far(tap_far, tf_send, tf_sem)

    edge.wait()
    tail_s[ROWS - 2 :, :] = tail_s[ROWS - 2 :, :] + jnp.where(me < n - 1, edge_recv[...], 0.0)
    grad_ref[span - ROWS :, :] = tail_s[...].astype(BF16)
    last = pl.ds(span - ROWS, ROWS)
    tail = pltpu.make_async_copy(grad_ref.at[last, :], grad_hbm.at[last, :], out_sem.at[1])
    tail.start()

    take_far(mode_two, mt_send, mt_sem)
    mode_three[mine] = sum_of(mode_two)
    send_near(lambda p: mode_three.at[mine], mode_three, mh_send, mh_sem)
    main.wait()
    tail.wait()
    take_near(mode_three, mh_send, mh_sem)
    for index in tiles:
        which, row, lane, slot, place = tile_of(index)
        row = PIECE + which * MODES + row
        total_ref[row : row + 8, lane : lane + LANES] = mode_three[slot, place : place + 8, :]
    take_far(tap_far, tf_send, tf_sem)
    total_ref[:PIECE, :] = sum_of(tap_far)


def hand_out(total_ref, grad_ref, grad_out, taps_out, table_out, res_out, decay_out):
    grad_out[...] = grad_ref[...]
    for s in range(3):
        table_out[s] = total_ref[4 * s : 4 * s + 4, :]
        taps_out[s] = total_ref[12 + 3 * s : 15 + 3 * s, :]
    res_out[...] = total_ref[PIECE : PIECE + MODES, :]
    decay_out[...] = total_ref[PIECE + MODES :, :]


def shards(n, near, groups, inputs, letters, letter_table, short_taps, residues, decay_rate, cotangent):
    span, width = inputs.shape[1:]
    chans = width // n
    wide = 4 if n % 8 == 0 else 2
    fixed = tables(span)
    nodes = fixed["nodes"]
    node_cols = np.broadcast_to(nodes[:, None], (NODES, chans)).astype(np.float32)
    vmem = pl.BlockSpec(memory_space=pltpu.VMEM)
    anywhere = pl.BlockSpec(memory_space=pl.ANY)
    dma = pltpu.SemaphoreType.DMA
    operands = [inputs[0], letters, letter_table, short_taps, residues.T, decay_rate.T, cotangent[0]] + [
        jnp.asarray(fixed[name]) for name in ("forward", "moments", "inverse", "spread", "response")
    ] + [jnp.asarray(node_cols)]
    several = wide * chans
    share = GRADS * chans // LANES // near
    scratch = [pltpu.VMEM(value.shape, value.dtype) for value in operands] + [
        pltpu.VMEM((ROWS, width), BF16),
        pltpu.VMEM((span + 2 * NODES, 2 * span), BF16),
        pltpu.VMEM((span, width), BF16),
        pltpu.VMEM((span + 8, width), F32),
        pltpu.VMEM((span, width), F32),
        pltpu.VMEM((span, width), F32),
        pltpu.VMEM((span, width), BF16),
        pltpu.VMEM((span, width), BF16),
        pltpu.VMEM((span, width), F32),
        pltpu.VMEM((span, width), F32),
        pltpu.VMEM((span, LANES), F32),
        pltpu.VMEM((ROWS, 3 * span), BF16),
        pltpu.VMEM((ROWS, width), F32),
        pltpu.VMEM((ROWS, width), F32),
        pltpu.VMEM((2 * span, width), F32),
        pltpu.VMEM((2 * span, width), F32),
        pltpu.VMEM((2 * span, several), F32),
        pltpu.VMEM((2, 2 * span, several), BF16),
        pltpu.VMEM((2, span, several), F32),
        pltpu.VMEM((3 * span, several), BF16),
        pltpu.VMEM((2, span + 8, chans), F32),
        pltpu.VMEM((ROWS, width), F32),
    ] + [pltpu.VMEM((NODES, MODES, chans), F32)] * 4 + [pltpu.VMEM((n, MODES, chans), F32)] * 6 + [
        pltpu.VMEM((2 * NODES, chans), F32),
        pltpu.VMEM((2, MODES, chans), F32),
    ] + [pltpu.VMEM((2, width), F32)] * 4 + [
        pltpu.VMEM((NODES, chans), BF16),
        pltpu.VMEM((n, NODES, chans), BF16),
        pltpu.VMEM((n, 2 * NODES, chans), BF16),
        pltpu.VMEM((n, 2 * NODES, chans), BF16),
        pltpu.VMEM((n, NODES, chans), F32),
        pltpu.VMEM((n, NODES, chans), F32),
        pltpu.VMEM((n, 2 * NODES, chans), BF16),
        pltpu.VMEM((n, 2 * NODES, chans), BF16),
        pltpu.VMEM((n, PIECE, chans), F32),
        pltpu.VMEM((n, PIECE, chans), F32),
        pltpu.VMEM((near, share, LANES), F32),
        pltpu.VMEM((near, share, LANES), F32),
        pltpu.VMEM((groups, share, LANES), F32),
        pltpu.VMEM((near, share, LANES), F32),
        pltpu.VMEM((near, PIECE, chans), F32),
        pltpu.VMEM((groups, PIECE, chans), F32),
        dma((len(operands) + 1,)),
        dma((2,)),
        dma((4,)),
    ] + [dma((n,))] * 10 + ([dma((near,))] * 2 + [dma((groups,))] * 2 + [dma((near,))] * 2) + [dma((near,))] * 2 + [dma((groups,))] * 2
    grad, total = pl.pallas_call(
        functools.partial(kernel, n, near, groups, wide, span, chans, nodes),
        out_shape=(
            jax.ShapeDtypeStruct((span, width), BF16),
            jax.ShapeDtypeStruct((PIECE + GRADS, chans), F32),
        ),
        in_specs=[anywhere] * len(operands),
        out_specs=(anywhere, vmem),
        scratch_shapes=scratch,
        compiler_params=pltpu.CompilerParams(
            collective_id=0, has_side_effects=True, vmem_limit_bytes=56 * 1024 * 1024
        ),
    )(*operands)
    grad, taps_grad, table_grad, residue_grad, decay_grad = pl.pallas_call(
        hand_out,
        out_shape=(
            jax.ShapeDtypeStruct((span, width), BF16),
            jax.ShapeDtypeStruct((3, 3, chans), F32),
            jax.ShapeDtypeStruct((3, 4, chans), F32),
            jax.ShapeDtypeStruct((MODES, chans), F32),
            jax.ShapeDtypeStruct((MODES, chans), F32),
        ),
        in_specs=[vmem] * 2,
        out_specs=(vmem,) * 5,
        compiler_params=pltpu.CompilerParams(vmem_limit_bytes=56 * 1024 * 1024),
    )(total, grad)
    return grad[None], taps_grad, table_grad, residue_grad.T, decay_grad.T


def solution(mesh):
    n, sequences = mesh.shape["ctx"], mesh.shape["dp"]
    near = max(k for k in (1, 2, 4, 8) if sequences % k == 0 and k * k <= 2 * sequences)
    in_specs = (
        P("dp", "ctx", None),
        P("dp", "ctx"),
        P(),
        P(),
        P("ctx", None),
        P("ctx", None),
        P("dp", "ctx", None),
    )
    out_specs = (
        P("dp", "ctx", None),
        P(None, None, "ctx"),
        P(None, None, "ctx"),
        P("ctx", None),
        P("ctx", None),
    )
    body = functools.partial(shards, n, near, sequences // near)
    return jax.shard_map(body, mesh=mesh, in_specs=in_specs, out_specs=out_specs, check_vma=False)
```

```python
import functools

import jax
import jax.numpy as jnp
import numpy as np
from jax import lax
from jax.experimental import pallas as pl
from jax.experimental.pallas import tpu as pltpu
from jax.sharding import PartitionSpec as P

MESH = pl.DeviceIdType.MESH
F32 = jnp.float32
BF16 = jnp.bfloat16
NODES = 16
MODES = 16
ROWS = 16
PIECE = 24
GRADS = 2 * MODES
LANES = 128


def split(values):
    high = values.astype(jnp.bfloat16)
    low = (values - high.astype(np.float64)).astype(jnp.bfloat16)
    return high, low


def tables(span):
    half = span / 2
    centre = (span - 1) / 2
    angles = np.pi * (2 * np.arange(NODES) + 1) / (2 * NODES)
    nodes = centre + half * np.cos(angles)
    places = np.arange(span)
    interp = np.ones((span, NODES))
    for k in range(NODES):
        for other in range(NODES):
            if other != k:
                interp[:, k] *= (places - nodes[other]) / (nodes[k] - nodes[other])
    theta = 2 * np.pi * (np.arange(span) + 0.5) / (2 * span)
    phase = theta[:, None] * places[None, :]
    forward = np.concatenate([np.cos(phase), -np.sin(phase)], axis=0)
    inverse = np.concatenate([np.cos(phase.T), -np.sin(phase.T)], axis=1) / span
    l_hi, l_lo = split(interp)
    w_hi, w_lo = split(forward @ interp)
    m_hi, m_lo = split(interp.T @ inverse)
    return dict(
        nodes=nodes,
        forward=forward.astype(jnp.bfloat16),
        moments=np.concatenate([l_hi.T, l_lo.T], axis=0),
        inverse=np.concatenate([inverse, m_hi.astype(np.float64), m_lo.astype(np.float64)], axis=0).astype(np.float32),
        spread=np.concatenate([l_hi, l_lo], axis=1),
        response=np.concatenate([w_hi, w_lo], axis=1),
    )


def packed(rows):
    half = rows.shape[1] // 2
    return jnp.concatenate(
        [rows[:16], jnp.concatenate([rows[16:, :half], rows[16:, half:]], axis=0)], axis=1
    ).astype(BF16)


def unpacked(block):
    wide = block.shape[1] // 3 * 2
    block = block.astype(F32)
    return jnp.concatenate(
        [block[:, :wide], jnp.concatenate([block[:8, wide:], block[8:, wide:]], axis=1)], axis=0
    )


def dot(left, right):
    return jnp.dot(left, right, preferred_element_type=F32)


def kernel(n, near, groups, wide, span, chans, nodes, *refs):
    (
        x_hbm, letters_hbm, table_hbm, taps_hbm, res_hbm, decay_hbm, cot_hbm,
        fwd_hbm, mom_hbm, inv_hbm, spread_hbm, resp_hbm, node_hbm,
        grad_hbm, total_ref,
        x_ref, letters_ref, table_ref, taps_ref, res_ref, decay_ref, cot_ref,
        fwd_ref, mom_ref, inv_ref, spread_ref, resp_ref, node_ref,
        x_last, inv_s, grad_ref, xs, key_s, value_s, mix_s, gate_s, conv_s, back_s,
        code_s, hot_t, tab_s, tap_s, spec_m, spec_g, spec_h, prod_s, far_s, fg_s, sums_s, w_s, tail_s,
        e_s, ep_s, gt_s, gr_s, a_s, r_s, s_s, u_s, al_s, rl_s, row_s, par_s,
        halo_stage, halo_recv, edge_stage, edge_recv,
        hn_stage, hn_recv, pq_stage, pq_recv, fgn_stage, fgn_recv,
        yz_stage, yz_recv, piece_stage, piece_recv,
        mode_stage, mode_one, mode_two, mode_three, tap_near, tap_far,
        in_sem, out_sem, edge_sem,
        hn_send, hn_sem, pq_send, pq_sem, fgn_send, fgn_sem, yz_send, yz_sem, piece_send, piece_sem,
        mo_send, mo_sem, mt_send, mt_sem, mh_send, mh_sem, tn_send, tn_sem, tf_send, tf_sem,
    ) = refs
    me = lax.axis_index("ctx")
    seq = lax.axis_index("dp")
    mine, block = lax.rem(seq, near), seq // near
    ahead, behind = lax.rem(me + 1, n), lax.rem(me + n - 1, n)
    sets = n // wide
    width = wide * chans
    chunks = span // ROWS

    def lanes(d):
        return pl.ds(pl.multiple_of(d * chans, chans), chans)

    def set_lanes(first):
        return pl.ds(pl.multiple_of(first * chans, width), width)

    def first_of(r):
        return lax.rem(me // wide + r, sets) * wide

    def to_ctx(source, target, send, recv, d):
        return pltpu.make_async_remote_copy(
            src_ref=source, dst_ref=target, send_sem=send, recv_sem=recv,
            device_id=(seq, d), device_id_type=MESH,
        )

    def to_dp(source, target, send, recv, p):
        return pltpu.make_async_remote_copy(
            src_ref=source, dst_ref=target, send_sem=send, recv_sem=recv,
            device_id=(p, me), device_id_type=MESH,
        )

    def send_others(first, stage, recv_buffer, send, recv):
        for g in range(wide):
            d = first + g

            @pl.when(d != me)
            def _():
                to_ctx(stage.at[d], recv_buffer.at[me], send.at[d], recv.at[me], d).start()

    def take_others(stage, recv_buffer, send, recv):
        def take(r, carry):
            d = lax.rem(me + r, n)
            to_ctx(stage.at[d], recv_buffer.at[d], send.at[d], recv.at[d], d).wait()
            return carry

        lax.fori_loop(1, n, take, 0)

    steps = near // 2
    along, side = seq // 2, lax.rem(seq, 2)
    places = near * groups // 2
    offsets = range(-((steps - 1) // 2), steps - (steps - 1) // 2)

    def at_offset(offset, other):
        return lax.rem(along + offset + places, places) * 2 + lax.rem(side + other, 2)

    def around_copies(index, offset, other):
        def outward():
            return to_dp(tap_near.at[mine], tap_near.at[mine], tn_send.at[index], tn_sem.at[mine], at_offset(-offset, other))

        def inward():
            slot = lax.rem(at_offset(offset, other), near)
            return to_dp(tap_near.at[slot], tap_near.at[slot], tn_send.at[index], tn_sem.at[slot], at_offset(offset, other))

        return outward, inward

    around = [
        around_copies(index, offset, other)
        for index, (offset, other) in enumerate((o, s) for o in offsets for s in range(2) if (o, s) != (0, 0))
    ]

    barrier = pltpu.get_barrier_semaphore()

    def greet_ctx(r, carry):
        pl.semaphore_signal(barrier, inc=1, device_id=(seq, lax.rem(me + r, n)), device_id_type=MESH)
        return carry

    def greet_near(r, carry):
        peer = block * near + lax.rem(mine + r, near)
        pl.semaphore_signal(barrier, inc=1, device_id=(peer, me), device_id_type=MESH)
        return carry

    def greet_far(r, carry):
        peer = lax.rem(block + r, groups) * near + mine
        pl.semaphore_signal(barrier, inc=1, device_id=(peer, me), device_id_type=MESH)
        return carry

    lax.fori_loop(1, n, greet_ctx, 0)
    lax.fori_loop(1, near, greet_near, 0)
    lax.fori_loop(1, groups, greet_far, 0)
    greeted = [(o, s) for o in sorted(set(offsets) | {-o for o in offsets}) for s in range(2) if (o, s) != (0, 0)]
    for offset, other in greeted:
        pl.semaphore_signal(barrier, inc=1, device_id=(at_offset(offset, other), me), device_id_type=MESH)

    loads = [
        pltpu.make_async_copy(source, target, in_sem.at[i])
        for i, (source, target) in enumerate([
            (x_hbm.at[pl.ds(span - ROWS, ROWS), :], x_last),
            (res_hbm, res_ref), (decay_hbm, decay_ref), (node_hbm, node_ref), (x_hbm, x_ref),
            (letters_hbm, letters_ref), (table_hbm, table_ref), (taps_hbm, taps_ref), (cot_hbm, cot_ref),
            (mom_hbm, mom_ref),
            (fwd_hbm, fwd_ref), (inv_hbm, inv_ref), (resp_hbm, resp_ref), (spread_hbm, spread_ref),
        ])
    ]
    for load in loads:
        load.start()
    for load in loads[1:4]:
        load.wait()
    rate, weight = decay_ref[...], res_ref[...]
    twice = 2.0 * rate
    series = 1.0 - twice * (1.0 / 7.0)
    for term in (6.0, 5.0, 4.0, 3.0, 2.0):
        series = 1.0 - twice * (1.0 / term) * series
    scale = jnp.sqrt(twice * series)
    gain = weight * scale
    par_s[0] = gain
    par_s[1] = scale
    node_col = node_ref[...]
    own_filter = jnp.zeros((NODES, chans), F32)
    for m in range(MODES):
        wave = par_s[0, m : m + 1, :] * jnp.exp(-decay_ref[m : m + 1, :] * node_col)
        gt_s[m] = wave
        own_filter = own_filter + wave
    hn_stage[...] = own_filter.astype(BF16)
    hn_recv[me] = own_filter.astype(BF16)

    for m in range(MODES):
        gr_s[m] = par_s[0, m : m + 1, :] * jnp.exp(-decay_ref[m : m + 1, :] * (float(span) - node_col))
    for k in range(NODES):
        e_s[k] = jnp.exp(-rate * float(nodes[k]))
        ep_s[k] = jnp.exp(-rate * float(span - nodes[k]))

    loads[0].wait()
    halo_stage[...] = x_last[...].astype(F32)[ROWS - 2 :, :]
    pl.semaphore_wait(barrier, (n - 1) + (near - 1) + (groups - 1) + len(greeted))
    halo = to_ctx(halo_stage, halo_recv, edge_sem.at[0], edge_sem.at[1], ahead)
    halo.start()

    def send_filter(r, carry):
        d = lax.rem(me + r, n)
        to_ctx(hn_stage, hn_recv.at[me], hn_send.at[d], hn_sem.at[me], d).start()
        return carry

    lax.fori_loop(1, n, send_filter, 0)
    for load in loads[4:9]:
        load.wait()

    codes = jnp.concatenate([letters_ref[...] + 4 * s for s in range(3)], axis=1)
    hot_t[...] = (lax.broadcasted_iota(jnp.int32, (ROWS, 3 * span), 0) == codes).astype(F32).astype(BF16)
    code_s[...] = jnp.transpose(jnp.broadcast_to(letters_ref[...].astype(F32), (LANES, span)))

    def products(at, which):
        tap = [tap_s[i : i + 1, at] for i in range(9)]
        tab = [tab_s[i : i + 1, at] for i in range(12)]
        for c in which:
            low = c * ROWS
            rows = slice(low, low + ROWS)
            code = code_s[rows, :]
            is_one, is_two, is_three = code == 1.0, code == 2.0, code == 3.0
            lag = [xs[8 + low - j : 8 + low - j + ROWS, at] for j in range(3)]
            stream = []
            for s in range(3):
                part = jnp.where(
                    is_one,
                    tab[4 * s + 1],
                    jnp.where(is_two, tab[4 * s + 2], jnp.where(is_three, tab[4 * s + 3], tab[4 * s])),
                )
                for j in range(3):
                    part = part + tap[3 * s + j] * lag[j]
                stream.append(part)
            key_s[rows, at] = stream[1]
            value_s[rows, at] = stream[2]
            mix_s[rows, at] = (stream[1] * stream[2]).astype(BF16)
            gate_s[rows, at] = (cot_ref[rows, at].astype(F32) * stream[0]).astype(BF16)

    def late_rows(g, carry):
        at = lanes(g)
        xs[8:, at] = x_ref[:, at].astype(F32)
        for s in range(3):
            tap_s[3 * s : 3 * s + 3, at] = taps_ref[s, :, at].astype(F32)
            tab_s[4 * s : 4 * s + 4, at] = table_ref[s, :, at].astype(F32)
        for t in range(chans // LANES):
            products(pl.ds(pl.multiple_of(g * chans + t * LANES, LANES), LANES), range(1, chunks))
        return carry

    lax.fori_loop(0, n, late_rows, 0)
    loads[9].wait()
    halo.wait()
    xs[6:8, :] = jnp.where(me > 0, halo_recv[...], 0.0)

    def node_sums(r, carry):
        first = first_of(r)
        for t in range(width // LANES):
            products(pl.ds(pl.multiple_of(first * chans + t * LANES, LANES), LANES), range(1))
        at = set_lanes(first)
        p_sum = dot(mom_ref[...], mix_s[:, at])
        q_sum = dot(mom_ref[...], gate_s[:, at])
        sums = jnp.concatenate([p_sum[:NODES] + p_sum[NODES:], q_sum[:NODES] + q_sum[NODES:]], axis=0).astype(BF16)
        for g in range(wide):
            pq_stage[first + g] = sums[:, g * chans : (g + 1) * chans]
        send_others(first, pq_stage, pq_recv, pq_send, pq_sem)
        return carry

    lax.fori_loop(1, sets + 1, node_sums, 0)
    pq_recv[me] = pq_stage[me]

    for load in loads[10:]:
        load.wait()
    inv_s[...] = inv_ref[...].astype(BF16)

    spec_m[...] = dot(fwd_ref[...], mix_s[...])
    spec_g[...] = dot(fwd_ref[...], gate_s[...])

    def correlate(t, carry):
        at = pl.ds(pl.multiple_of(t * LANES, LANES), LANES)
        for c in range(chunks):
            re, im = slice(c * ROWS, c * ROWS + ROWS), slice(span + c * ROWS, span + c * ROWS + ROWS)
            mr, mi = spec_m[re, at], spec_m[im, at]
            gr, gi = spec_g[re, at], spec_g[im, at]
            prod_s[0, re, at] = (gr * mr + gi * mi).astype(BF16)
            prod_s[0, im, at] = (gi * mr - gr * mi).astype(BF16)
        return carry

    lax.fori_loop(0, n * chans // LANES, correlate, 0)
    both = dot(inv_s[span:, :], prod_s[0])
    sums = both[:NODES] + both[NODES:]
    for d in range(n):
        fgn_stage[d] = sums[:, d * chans : (d + 1) * chans]

    def send_correlation(r, carry):
        d = lax.rem(me + r, n)
        to_ctx(fgn_stage.at[d], fgn_recv.at[me], fgn_send.at[d], fgn_sem.at[me], d).start()
        return carry

    lax.fori_loop(1, n, send_correlation, 0)

    def take_filter(r, carry):
        d = lax.rem(me + r, n)
        to_ctx(hn_stage, hn_recv.at[d], hn_send.at[d], hn_sem.at[d], d).wait()
        return carry

    lax.fori_loop(1, n, take_filter, 0)

    own = jnp.concatenate([hn_recv[d] for d in range(n)], axis=1)
    spec_h[...] = dot(resp_ref[...], jnp.concatenate([own, own], axis=0))

    take_others(pq_stage, pq_recv, pq_send, pq_sem)

    def weigh(buffer, rows, k, table, sums):
        return [total + buffer[i, rows + k : rows + k + 1, :] * table[k] for i, total in enumerate(sums)]

    def states(j, carry):
        for i in range(2):
            row_s[i] = pq_recv[2 * j + i].astype(F32)
        a_sums = [jnp.zeros((MODES, chans), F32) for _ in range(2)]
        r_sums = [jnp.zeros((MODES, chans), F32) for _ in range(2)]
        for k in range(NODES):
            a_sums = weigh(row_s, 0, k, ep_s, a_sums)
            r_sums = weigh(row_s, NODES, k, e_s, r_sums)
        for i in range(2):
            a_s[2 * j + i] = a_sums[i]
            r_s[2 * j + i] = r_sums[i]
        return carry

    lax.fori_loop(0, n // 2, states, 0)
    step = jnp.exp(-decay_ref[...] * float(span))

    def recur(i, carry):
        forward_state, backward_state = carry
        s_s[i] = forward_state
        u_s[n - 1 - i] = backward_state
        return step * forward_state + a_s[i], step * backward_state + r_s[n - 1 - i]

    nothing = jnp.zeros((MODES, chans), F32)
    lax.fori_loop(0, n, recur, (nothing, nothing))

    def respond(r, carry):
        pair_of = [lax.rem(me // 2 * 2 + 2 * r + i, n) for i in range(2)]
        y_sums = [jnp.zeros((NODES, chans), F32) for _ in range(2)]
        z_sums = [jnp.zeros((NODES, chans), F32) for _ in range(2)]
        for m in range(MODES):
            y_sums = [total + s_s[d, m : m + 1, :] * gt_s[m] for d, total in zip(pair_of, y_sums)]
            z_sums = [total + u_s[d, m : m + 1, :] * gr_s[m] for d, total in zip(pair_of, z_sums)]
        for i in range(2):
            yz_stage[pair_of[i]] = jnp.concatenate([y_sums[i], z_sums[i]], axis=0).astype(BF16)
        for d in pair_of:

            @pl.when(d != me)
            def _():
                to_ctx(yz_stage.at[d], yz_recv.at[me], yz_send.at[d], yz_sem.at[me], d).start()

        return carry

    lax.fori_loop(1, n // 2 + 1, respond, 0)
    yz_recv[me] = yz_stage[me]

    def inside(t, carry):
        at = pl.ds(pl.multiple_of(t * LANES, LANES), LANES)
        for c in range(chunks):
            re, im = slice(c * ROWS, c * ROWS + ROWS), slice(span + c * ROWS, span + c * ROWS + ROWS)
            hr, hi = spec_h[re, at], spec_h[im, at]
            mr, mi = spec_m[re, at], spec_m[im, at]
            gr, gi = spec_g[re, at], spec_g[im, at]
            prod_s[0, re, at] = (hr * mr - hi * mi).astype(BF16)
            prod_s[0, im, at] = (hr * mi + hi * mr).astype(BF16)
            prod_s[1, re, at] = (hr * gr + hi * gi).astype(BF16)
            prod_s[1, im, at] = (hr * gi - hi * gr).astype(BF16)
        return carry

    lax.fori_loop(0, n * chans // LANES, inside, 0)
    conv_s[...] = dot(inv_s[:span, :], prod_s[0])
    back_s[...] = dot(inv_s[:span, :], prod_s[1])

    def lags(j, carry):
        for i in range(2):
            sums = pq_recv[2 * j + i].astype(F32)
            row_s[i, :NODES] = sums[:NODES] * (float(span) - node_ref[...])
            row_s[i, NODES:] = sums[NODES:] * node_ref[...]
        a_sums = [jnp.zeros((MODES, chans), F32) for _ in range(2)]
        r_sums = [jnp.zeros((MODES, chans), F32) for _ in range(2)]
        for k in range(NODES):
            a_sums = weigh(row_s, 0, k, ep_s, a_sums)
            r_sums = weigh(row_s, NODES, k, e_s, r_sums)
        for i in range(2):
            al_s[2 * j + i] = a_sums[i]
            rl_s[2 * j + i] = r_sums[i]
        return carry

    lax.fori_loop(0, n // 2, lags, 0)

    def pair(i, carry):
        lag_state, exp_sum, lag_sum = carry
        state, reach = s_s[i], r_s[i]
        exp_sum = exp_sum + reach * state
        lag_sum = lag_sum + rl_s[i] * state + reach * lag_state
        return step * (lag_state + float(span) * state) + al_s[i], exp_sum, lag_sum

    _, exp_sum, lag_sum = lax.fori_loop(0, n, pair, (nothing, nothing, nothing))
    take_others(fgn_stage, fgn_recv, fgn_send, fgn_sem)
    fgn_recv[me] = fgn_stage[me]
    near_sum = fgn_recv[0]
    for d in range(1, n):
        near_sum = near_sum + fgn_recv[d]
    row_s[0, :NODES] = near_sum
    row_s[0, NODES:] = near_sum * node_ref[...]
    for k in range(NODES):
        exp_sum = exp_sum + row_s[0, k : k + 1, :] * e_s[k]
        lag_sum = lag_sum + row_s[0, NODES + k : NODES + k + 1, :] * e_s[k]
    mode_grads = (
        par_s[1] * exp_sum,
        res_ref[...] * jnp.exp(-2.0 * decay_ref[...]) / par_s[1] * exp_sum - par_s[0] * lag_sum,
    )

    def tile_of(index):
        row, lane = index // (chans // LANES), index % (chans // LANES)
        per = GRADS // 8 * (chans // LANES) // near
        return row // 2, row % 2 * 8, lane * LANES, index // per, index % per * 8

    tiles = range(GRADS // 8 * (chans // LANES))
    for index in tiles:
        which, row, lane, slot, place = tile_of(index)
        mode_stage[slot, place : place + 8, :] = mode_grads[which][row : row + 8, lane : lane + LANES]

    def send_near(source, target, send, recv):
        def one(r, carry):
            p = lax.rem(mine + r, near)
            to_dp(source(p), target.at[mine], send.at[p], recv.at[mine], block * near + p).start()
            return carry

        lax.fori_loop(1, near, one, 0)

    def take_near(target, send, recv):
        def one(r, carry):
            p = lax.rem(mine + r, near)
            to_dp(target.at[p], target.at[p], send.at[p], recv.at[p], block * near + p).wait()
            return carry

        lax.fori_loop(1, near, one, 0)

    def send_far(target, send, recv):
        def one(r, carry):
            b = lax.rem(block + r, groups)
            to_dp(target.at[block], target.at[block], send.at[b], recv.at[block], b * near + mine).start()
            return carry

        lax.fori_loop(1, groups, one, 0)

    def take_far(target, send, recv):
        def one(r, carry):
            b = lax.rem(block + r, groups)
            to_dp(target.at[b], target.at[b], send.at[b], recv.at[b], b * near + mine).wait()
            return carry

        lax.fori_loop(1, groups, one, 0)

    def sum_of(buffer):
        total = buffer[0]
        for p in range(1, buffer.shape[0]):
            total = total + buffer[p]
        return total

    send_near(lambda p: mode_stage.at[p], mode_one, mo_send, mo_sem)
    mode_one[mine] = mode_stage[mine]

    take_others(yz_stage, yz_recv, yz_send, yz_sem)
    for which in range(2):
        rows = slice(which * NODES, (which + 1) * NODES)
        node = jnp.concatenate([yz_recv[d, rows] for d in range(n)], axis=1)
        far_s[which] = dot(spread_ref[...], jnp.concatenate([node, node], axis=0))

    def finish(r, carry):
        first = first_of(r)

        def gradients(g, carry):
            for t in range(chans // LANES):
                some = pl.ds(pl.multiple_of(g * chans + t * LANES, LANES), LANES)
                at = pl.ds(pl.multiple_of((first + g) * chans + t * LANES, LANES), LANES)
                totals = [jnp.zeros((8, LANES), F32) for _ in range(9)]
                for c in range(chunks):
                    low = c * ROWS
                    rows = slice(low, low + ROWS)
                    conv = (conv_s[rows, at] + far_s[0, rows, at]).astype(BF16).astype(F32)
                    back = (back_s[rows, at] + far_s[1, rows, at]).astype(BF16).astype(F32)
                    conv_s[rows, at] = conv
                    back_s[rows, at] = back
                    grads = [
                        cot_ref[rows, at].astype(F32) * conv,
                        back * value_s[rows, at],
                        back * key_s[rows, at],
                    ]
                    lag = [xs[8 + low - j : 8 + low - j + ROWS, at] for j in range(3)]
                    for s in range(3):
                        fg_s[s * span + low : s * span + low + ROWS, some] = grads[s].astype(BF16)
                        for j in range(3):
                            part = grads[s] * lag[j]
                            totals[3 * s + j] = totals[3 * s + j] + (part[:8] + part[8:])
                for i in range(9):
                    sums_s[g, 12 + i : 13 + i, t * LANES : (t + 1) * LANES] = jnp.sum(totals[i], axis=0, keepdims=True)
            return carry

        lax.fori_loop(0, wide, gradients, 0)
        letter_sums = dot(hot_t[...], fg_s[...])
        for g in range(wide):
            sums_s[g, :12, :] = letter_sums[:12, g * chans : (g + 1) * chans]
            sums_s[g, 21:, :] = jnp.zeros((PIECE - 21, chans), F32)
            piece_stage[first + g] = packed(sums_s[g])
        send_others(first, piece_stage, piece_recv, piece_send, piece_sem)
        return carry

    lax.fori_loop(1, sets + 1, finish, 0)

    take_near(mode_one, mo_send, mo_sem)
    mode_two[block] = sum_of(mode_one)
    send_far(mode_two, mt_send, mt_sem)

    take_others(piece_stage, piece_recv, piece_send, piece_sem)
    piece_recv[me] = piece_stage[me]
    piece = piece_recv[0].astype(F32)
    for d in range(1, n):
        piece = piece + piece_recv[d].astype(F32)
    tap_far[block] = unpacked(piece)
    send_far(tap_far, tf_send, tf_sem)

    w_s[0, span : span + 8, :] = jnp.zeros((8, chans), F32)
    w_s[1, span : span + 8, :] = jnp.zeros((8, chans), F32)

    def input_gradient(d, carry):
        for t in range(chans // LANES):
            some = slice(t * LANES, (t + 1) * LANES)
            at = pl.ds(pl.multiple_of(d * chans + t * LANES, LANES), LANES)
            tap = [tap_s[i : i + 1, at] for i in range(9)]
            for c in reversed(range(chunks)):
                low = c * ROWS
                rows = slice(low, low + ROWS)
                back = back_s[rows, at]
                grads = [cot_ref[rows, at].astype(F32) * conv_s[rows, at], back * value_s[rows, at], back * key_s[rows, at]]
                ahead_by = [tap[j] * grads[0] + tap[3 + j] * grads[1] + tap[6 + j] * grads[2] for j in range(3)]
                w_s[0, rows, some] = ahead_by[1]
                w_s[1, rows, some] = ahead_by[2]
                part = (
                    ahead_by[0]
                    + w_s[0, low + 1 : low + 1 + ROWS, some]
                    + w_s[1, low + 2 : low + 2 + ROWS, some]
                )
                if c < chunks - 1:
                    grad_ref[rows, at] = part.astype(BF16)
                else:
                    tail_s[:, at] = part
            edge_stage[0:1, at] = w_s[1, 0:1, some]
            edge_stage[1:2, at] = w_s[0, 0:1, some] + w_s[1, 1:2, some]
        return carry

    lax.fori_loop(0, n, input_gradient, 0)
    edge = to_ctx(edge_stage, edge_recv, edge_sem.at[2], edge_sem.at[3], behind)
    edge.start()
    body = pl.ds(0, span - ROWS)
    main = pltpu.make_async_copy(grad_ref.at[body, :], grad_hbm.at[body, :], out_sem.at[0])
    main.start()

    edge.wait()
    tail_s[ROWS - 2 :, :] = tail_s[ROWS - 2 :, :] + jnp.where(me < n - 1, edge_recv[...], 0.0)
    grad_ref[span - ROWS :, :] = tail_s[...].astype(BF16)
    last = pl.ds(span - ROWS, ROWS)
    tail = pltpu.make_async_copy(grad_ref.at[last, :], grad_hbm.at[last, :], out_sem.at[1])
    tail.start()

    take_far(mode_two, mt_send, mt_sem)
    mode_three[mine] = sum_of(mode_two)
    send_near(lambda p: mode_three.at[mine], mode_three, mh_send, mh_sem)
    take_far(tap_far, tf_send, tf_sem)
    tap_near[mine] = sum_of(tap_far)
    for copy, _ in around:
        copy().start()
    main.wait()
    tail.wait()
    take_near(mode_three, mh_send, mh_sem)
    for index in tiles:
        which, row, lane, slot, place = tile_of(index)
        row = PIECE + which * MODES + row
        total_ref[row : row + 8, lane : lane + LANES] = mode_three[slot, place : place + 8, :]
    for _, copy in around:
        copy().wait()
    total_ref[:PIECE, :] = sum_of(tap_near)


def hand_out(total_ref, grad_ref, grad_out, taps_out, table_out, res_out, decay_out):
    grad_out[...] = grad_ref[...]
    for s in range(3):
        table_out[s] = total_ref[4 * s : 4 * s + 4, :]
        taps_out[s] = total_ref[12 + 3 * s : 15 + 3 * s, :]
    res_out[...] = total_ref[PIECE : PIECE + MODES, :]
    decay_out[...] = total_ref[PIECE + MODES :, :]


def shards(n, near, groups, inputs, letters, letter_table, short_taps, residues, decay_rate, cotangent):
    span, width = inputs.shape[1:]
    chans = width // n
    wide = 4 if n % 8 == 0 else 2
    fixed = tables(span)
    nodes = fixed["nodes"]
    node_cols = np.broadcast_to(nodes[:, None], (NODES, chans)).astype(np.float32)
    vmem = pl.BlockSpec(memory_space=pltpu.VMEM)
    anywhere = pl.BlockSpec(memory_space=pl.ANY)
    dma = pltpu.SemaphoreType.DMA
    operands = [inputs[0], letters, letter_table, short_taps, residues.T, decay_rate.T, cotangent[0]] + [
        jnp.asarray(fixed[name]) for name in ("forward", "moments", "inverse", "spread", "response")
    ] + [jnp.asarray(node_cols)]
    several = wide * chans
    share = GRADS * chans // LANES // near
    scratch = [pltpu.VMEM(value.shape, value.dtype) for value in operands] + [
        pltpu.VMEM((ROWS, width), BF16),
        pltpu.VMEM((span + 2 * NODES, 2 * span), BF16),
        pltpu.VMEM((span, width), BF16),
        pltpu.VMEM((span + 8, width), F32),
        pltpu.VMEM((span, width), F32),
        pltpu.VMEM((span, width), F32),
        pltpu.VMEM((span, width), BF16),
        pltpu.VMEM((span, width), BF16),
        pltpu.VMEM((span, width), F32),
        pltpu.VMEM((span, width), F32),
        pltpu.VMEM((span, LANES), F32),
        pltpu.VMEM((ROWS, 3 * span), BF16),
        pltpu.VMEM((ROWS, width), F32),
        pltpu.VMEM((ROWS, width), F32),
        pltpu.VMEM((2 * span, width), F32),
        pltpu.VMEM((2 * span, width), F32),
        pltpu.VMEM((2 * span, width), F32),
        pltpu.VMEM((2, 2 * span, width), BF16),
        pltpu.VMEM((2, span, width), F32),
        pltpu.VMEM((3 * span, several), BF16),
        pltpu.VMEM((wide, PIECE, chans), F32),
        pltpu.VMEM((2, span + 8, chans), F32),
        pltpu.VMEM((ROWS, width), F32),
    ] + [pltpu.VMEM((NODES, MODES, chans), F32)] * 4 + [pltpu.VMEM((n, MODES, chans), F32)] * 6 + [
        pltpu.VMEM((2, 2 * NODES, chans), F32),
        pltpu.VMEM((2, MODES, chans), F32),
    ] + [pltpu.VMEM((2, width), F32)] * 4 + [
        pltpu.VMEM((NODES, chans), BF16),
        pltpu.VMEM((n, NODES, chans), BF16),
        pltpu.VMEM((n, 2 * NODES, chans), BF16),
        pltpu.VMEM((n, 2 * NODES, chans), BF16),
        pltpu.VMEM((n, NODES, chans), F32),
        pltpu.VMEM((n, NODES, chans), F32),
        pltpu.VMEM((n, 2 * NODES, chans), BF16),
        pltpu.VMEM((n, 2 * NODES, chans), BF16),
        pltpu.VMEM((n, 16, chans * 3 // 2), BF16),
        pltpu.VMEM((n, 16, chans * 3 // 2), BF16),
        pltpu.VMEM((near, share, LANES), F32),
        pltpu.VMEM((near, share, LANES), F32),
        pltpu.VMEM((groups, share, LANES), F32),
        pltpu.VMEM((near, share, LANES), F32),
        pltpu.VMEM((near, PIECE, chans), F32),
        pltpu.VMEM((groups, PIECE, chans), F32),
        dma((len(operands) + 1,)),
        dma((2,)),
        dma((4,)),
    ] + [dma((n,))] * 10 + ([dma((near,))] * 2 + [dma((groups,))] * 2 + [dma((near,))] * 2) + [dma((near,))] * 2 + [dma((groups,))] * 2
    grad, total = pl.pallas_call(
        functools.partial(kernel, n, near, groups, wide, span, chans, nodes),
        out_shape=(
            jax.ShapeDtypeStruct((span, width), BF16),
            jax.ShapeDtypeStruct((PIECE + GRADS, chans), F32),
        ),
        in_specs=[anywhere] * len(operands),
        out_specs=(anywhere, vmem),
        scratch_shapes=scratch,
        compiler_params=pltpu.CompilerParams(
            collective_id=0, has_side_effects=True, vmem_limit_bytes=56 * 1024 * 1024
        ),
    )(*operands)
    grad, taps_grad, table_grad, residue_grad, decay_grad = pl.pallas_call(
        hand_out,
        out_shape=(
            jax.ShapeDtypeStruct((span, width), BF16),
            jax.ShapeDtypeStruct((3, 3, chans), F32),
            jax.ShapeDtypeStruct((3, 4, chans), F32),
            jax.ShapeDtypeStruct((MODES, chans), F32),
            jax.ShapeDtypeStruct((MODES, chans), F32),
        ),
        in_specs=[vmem] * 2,
        out_specs=(vmem,) * 5,
        compiler_params=pltpu.CompilerParams(vmem_limit_bytes=56 * 1024 * 1024),
    )(total, grad)
    return grad[None], taps_grad, table_grad, residue_grad.T, decay_grad.T


def solution(mesh):
    n, sequences = mesh.shape["ctx"], mesh.shape["dp"]
    near = max(k for k in (1, 2, 4, 8) if sequences % k == 0 and k * k <= 2 * sequences)
    in_specs = (
        P("dp", "ctx", None),
        P("dp", "ctx"),
        P(),
        P(),
        P("ctx", None),
        P("ctx", None),
        P("dp", "ctx", None),
    )
    out_specs = (
        P("dp", "ctx", None),
        P(None, None, "ctx"),
        P(None, None, "ctx"),
        P("ctx", None),
        P("ctx", None),
    )
    body = functools.partial(shards, n, near, sequences // near)
    return jax.shard_map(body, mesh=mesh, in_specs=in_specs, out_specs=out_specs, check_vma=False)
```

```python
import functools

import jax
import jax.numpy as jnp
import numpy as np
from jax import lax
from jax.experimental import pallas as pl
from jax.experimental.pallas import tpu as pltpu
from jax.sharding import PartitionSpec as P

MESH = pl.DeviceIdType.MESH
F32 = jnp.float32
BF16 = jnp.bfloat16
NODES = 16
MODES = 16
ROWS = 16
PIECE = 24
GRADS = 2 * MODES
LANES = 128


def split(values):
    high = values.astype(jnp.bfloat16)
    low = (values - high.astype(np.float64)).astype(jnp.bfloat16)
    return high, low


def tables(span):
    half = span / 2
    centre = (span - 1) / 2
    angles = np.pi * (2 * np.arange(NODES) + 1) / (2 * NODES)
    nodes = centre + half * np.cos(angles)
    places = np.arange(span)
    interp = np.ones((span, NODES))
    for k in range(NODES):
        for other in range(NODES):
            if other != k:
                interp[:, k] *= (places - nodes[other]) / (nodes[k] - nodes[other])
    theta = 2 * np.pi * (np.arange(span) + 0.5) / (2 * span)
    phase = theta[:, None] * places[None, :]
    forward = np.concatenate([np.cos(phase), -np.sin(phase)], axis=0)
    inverse = np.concatenate([np.cos(phase.T), -np.sin(phase.T)], axis=1) / span
    l_hi, l_lo = split(interp)
    w_hi, w_lo = split(forward @ interp)
    m_hi, m_lo = split(interp.T @ inverse)
    return dict(
        nodes=nodes,
        forward=forward.astype(jnp.bfloat16),
        moments=np.concatenate([l_hi.T, l_lo.T], axis=0),
        inverse=np.concatenate([inverse, m_hi.astype(np.float64), m_lo.astype(np.float64)], axis=0).astype(np.float32),
        spread=np.concatenate([l_hi, l_lo], axis=1),
        response=np.concatenate([w_hi, w_lo], axis=1),
    )


def packed(rows):
    half = rows.shape[1] // 2
    return jnp.concatenate(
        [rows[:16], jnp.concatenate([rows[16:, :half], rows[16:, half:]], axis=0)], axis=1
    ).astype(BF16)


def unpacked(block):
    wide = block.shape[1] // 3 * 2
    block = block.astype(F32)
    return jnp.concatenate(
        [block[:, :wide], jnp.concatenate([block[:8, wide:], block[8:, wide:]], axis=1)], axis=0
    )


def dot(left, right):
    return jnp.dot(left, right, preferred_element_type=F32)


def kernel(n, near, groups, wide, span, chans, nodes, *refs):
    (
        x_hbm, letters_hbm, table_hbm, taps_hbm, res_hbm, decay_hbm, cot_hbm,
        fwd_hbm, mom_hbm, inv_hbm, spread_hbm, resp_hbm, node_hbm,
        grad_hbm, total_ref,
        x_ref, letters_ref, table_ref, taps_ref, res_ref, decay_ref, cot_ref,
        fwd_ref, mom_ref, inv_ref, spread_ref, resp_ref, node_ref,
        x_last, inv_s, grad_ref, xs, key_s, value_s, mix_s, gate_s, conv_s, back_s,
        code_s, hot_t, tab_s, tap_s, spec_m, spec_g, spec_h, prod_s, far_s, fg_s, sums_s, w_s, tail_s,
        e_s, ep_s, gt_s, gr_s, a_s, r_s, s_s, u_s, al_s, rl_s, row_s, par_s,
        halo_stage, halo_recv, edge_stage, edge_recv,
        hn_stage, hn_recv, pq_stage, pq_recv, fgn_stage, fgn_recv,
        yz_stage, yz_recv, piece_stage, piece_recv,
        mode_stage, mode_one, mode_two, mode_three, tap_near, tap_far,
        in_sem, out_sem, edge_sem,
        hn_send, hn_sem, pq_send, pq_sem, fgn_send, fgn_sem, yz_send, yz_sem, piece_send, piece_sem,
        mo_send, mo_sem, mt_send, mt_sem, mh_send, mh_sem, tn_send, tn_sem, tf_send, tf_sem,
    ) = refs
    me = lax.axis_index("ctx")
    seq = lax.axis_index("dp")
    mine, block = lax.rem(seq, near), seq // near
    ahead, behind = lax.rem(me + 1, n), lax.rem(me + n - 1, n)
    sets = n // wide
    width = wide * chans
    chunks = span // ROWS

    def lanes(d):
        return pl.ds(pl.multiple_of(d * chans, chans), chans)

    def set_lanes(first):
        return pl.ds(pl.multiple_of(first * chans, width), width)

    def across(position, r, count):
        side_size = count // 2
        side = lax.rem(position // side_size + 1 - (r - 1) // side_size, 2)
        return side * side_size + lax.rem(position + r, side_size)

    def first_of(r):
        return across(me // wide, r, sets) * wide if sets > 1 else 0

    def to_ctx(source, target, send, recv, d):
        return pltpu.make_async_remote_copy(
            src_ref=source, dst_ref=target, send_sem=send, recv_sem=recv,
            device_id=(seq, d), device_id_type=MESH,
        )

    def to_dp(source, target, send, recv, p):
        return pltpu.make_async_remote_copy(
            src_ref=source, dst_ref=target, send_sem=send, recv_sem=recv,
            device_id=(p, me), device_id_type=MESH,
        )

    def send_others(first, stage, recv_buffer, send, recv):
        for g in range(wide):
            d = first + g

            @pl.when(d != me)
            def _():
                to_ctx(stage.at[d], recv_buffer.at[me], send.at[d], recv.at[me], d).start()

    def take_others(stage, recv_buffer, send, recv):
        def take(r, carry):
            d = lax.rem(me + r, n)
            to_ctx(stage.at[d], recv_buffer.at[d], send.at[d], recv.at[d], d).wait()
            return carry

        lax.fori_loop(1, n, take, 0)

    steps = near // 2
    along, side = seq // 2, lax.rem(seq, 2)
    places = near * groups // 2
    offsets = range(-((steps - 1) // 2), steps - (steps - 1) // 2)

    def at_offset(offset, other):
        return lax.rem(along + offset + places, places) * 2 + lax.rem(side + other, 2)

    def around_copies(index, offset, other):
        def outward():
            return to_dp(tap_near.at[mine], tap_near.at[mine], tn_send.at[index], tn_sem.at[mine], at_offset(-offset, other))

        def inward():
            slot = lax.rem(at_offset(offset, other), near)
            return to_dp(tap_near.at[slot], tap_near.at[slot], tn_send.at[index], tn_sem.at[slot], at_offset(offset, other))

        return outward, inward

    around = [
        around_copies(index, offset, other)
        for index, (offset, other) in enumerate((o, s) for o in sorted(offsets, key=abs, reverse=True) for s in (1, 0) if (o, s) != (0, 0))
    ]

    barrier = pltpu.get_barrier_semaphore()

    def greet_ctx(r, carry):
        pl.semaphore_signal(barrier, inc=1, device_id=(seq, lax.rem(me + r, n)), device_id_type=MESH)
        return carry

    def greet_near(r, carry):
        peer = block * near + lax.rem(mine + r, near)
        pl.semaphore_signal(barrier, inc=1, device_id=(peer, me), device_id_type=MESH)
        return carry

    def greet_far(r, carry):
        peer = lax.rem(block + r, groups) * near + mine
        pl.semaphore_signal(barrier, inc=1, device_id=(peer, me), device_id_type=MESH)
        return carry

    lax.fori_loop(1, n, greet_ctx, 0)
    lax.fori_loop(1, near, greet_near, 0)
    lax.fori_loop(1, groups, greet_far, 0)
    greeted = [(o, s) for o in sorted(set(offsets) | {-o for o in offsets}) for s in range(2) if (o, s) != (0, 0)]
    for offset, other in greeted:
        pl.semaphore_signal(barrier, inc=1, device_id=(at_offset(offset, other), me), device_id_type=MESH)

    loads = [
        pltpu.make_async_copy(source, target, in_sem.at[i])
        for i, (source, target) in enumerate([
            (x_hbm.at[pl.ds(span - ROWS, ROWS), :], x_last),
            (res_hbm, res_ref), (decay_hbm, decay_ref), (node_hbm, node_ref), (x_hbm, x_ref),
            (letters_hbm, letters_ref), (table_hbm, table_ref), (taps_hbm, taps_ref), (cot_hbm, cot_ref),
            (mom_hbm, mom_ref),
            (fwd_hbm, fwd_ref), (inv_hbm, inv_ref), (resp_hbm, resp_ref), (spread_hbm, spread_ref),
        ])
    ]
    for load in loads:
        load.start()
    for load in loads[1:4]:
        load.wait()
    rate, weight = decay_ref[...], res_ref[...]
    twice = 2.0 * rate
    series = 1.0 - twice * (1.0 / 7.0)
    for term in (6.0, 5.0, 4.0, 3.0, 2.0):
        series = 1.0 - twice * (1.0 / term) * series
    scale = jnp.sqrt(twice * series)
    gain = weight * scale
    par_s[0] = gain
    par_s[1] = scale
    node_col = node_ref[...]
    own_filter = jnp.zeros((NODES, chans), F32)
    for m in range(MODES):
        wave = par_s[0, m : m + 1, :] * jnp.exp(-decay_ref[m : m + 1, :] * node_col)
        gt_s[m] = wave
        own_filter = own_filter + wave
    hn_stage[...] = own_filter.astype(BF16)
    hn_recv[me] = own_filter.astype(BF16)

    for m in range(MODES):
        gr_s[m] = par_s[0, m : m + 1, :] * jnp.exp(-decay_ref[m : m + 1, :] * (float(span) - node_col))
    for k in range(NODES):
        e_s[k] = jnp.exp(-rate * float(nodes[k]))
        ep_s[k] = jnp.exp(-rate * float(span - nodes[k]))

    loads[0].wait()
    halo_stage[...] = x_last[...].astype(F32)[ROWS - 2 :, :]
    pl.semaphore_wait(barrier, (n - 1) + (near - 1) + (groups - 1) + len(greeted))
    halo = to_ctx(halo_stage, halo_recv, edge_sem.at[0], edge_sem.at[1], ahead)
    halo.start()

    def send_filter(r, carry):
        d = lax.rem(me + r, n)
        to_ctx(hn_stage, hn_recv.at[me], hn_send.at[d], hn_sem.at[me], d).start()
        return carry

    lax.fori_loop(1, n, send_filter, 0)
    for load in loads[4:9]:
        load.wait()

    codes = jnp.concatenate([letters_ref[...] + 4 * s for s in range(3)], axis=1)
    hot_t[...] = (lax.broadcasted_iota(jnp.int32, (ROWS, 3 * span), 0) == codes).astype(F32).astype(BF16)
    code_s[...] = jnp.transpose(jnp.broadcast_to(letters_ref[...].astype(F32), (LANES, span)))

    def products(at, which):
        tap = [tap_s[i : i + 1, at] for i in range(9)]
        tab = [tab_s[i : i + 1, at] for i in range(12)]
        for c in which:
            low = c * ROWS
            rows = slice(low, low + ROWS)
            code = code_s[rows, :]
            is_one, is_two, is_three = code == 1.0, code == 2.0, code == 3.0
            lag = [xs[8 + low - j : 8 + low - j + ROWS, at] for j in range(3)]
            stream = []
            for s in range(3):
                part = jnp.where(
                    is_one,
                    tab[4 * s + 1],
                    jnp.where(is_two, tab[4 * s + 2], jnp.where(is_three, tab[4 * s + 3], tab[4 * s])),
                )
                for j in range(3):
                    part = part + tap[3 * s + j] * lag[j]
                stream.append(part)
            key_s[rows, at] = stream[1]
            value_s[rows, at] = stream[2]
            mix_s[rows, at] = (stream[1] * stream[2]).astype(BF16)
            gate_s[rows, at] = (cot_ref[rows, at].astype(F32) * stream[0]).astype(BF16)

    def late_rows(g, carry):
        at = lanes(g)
        xs[8:, at] = x_ref[:, at].astype(F32)
        for s in range(3):
            tap_s[3 * s : 3 * s + 3, at] = taps_ref[s, :, at].astype(F32)
            tab_s[4 * s : 4 * s + 4, at] = table_ref[s, :, at].astype(F32)
        for t in range(chans // LANES):
            products(pl.ds(pl.multiple_of(g * chans + t * LANES, LANES), LANES), range(1, chunks))
        return carry

    lax.fori_loop(0, n, late_rows, 0)
    loads[9].wait()
    halo.wait()
    xs[6:8, :] = jnp.where(me > 0, halo_recv[...], 0.0)

    def node_sums(r, carry):
        first = first_of(r)
        for t in range(width // LANES):
            products(pl.ds(pl.multiple_of(first * chans + t * LANES, LANES), LANES), range(1))
        at = set_lanes(first)
        p_sum = dot(mom_ref[...], mix_s[:, at])
        q_sum = dot(mom_ref[...], gate_s[:, at])
        sums = jnp.concatenate([p_sum[:NODES] + p_sum[NODES:], q_sum[:NODES] + q_sum[NODES:]], axis=0).astype(BF16)
        for g in range(wide):
            pq_stage[first + g] = sums[:, g * chans : (g + 1) * chans]
        send_others(first, pq_stage, pq_recv, pq_send, pq_sem)
        return carry

    lax.fori_loop(1, sets + 1, node_sums, 0)
    pq_recv[me] = pq_stage[me]

    for load in loads[10:]:
        load.wait()
    inv_s[...] = inv_ref[...].astype(BF16)

    spec_m[...] = dot(fwd_ref[...], mix_s[...])
    spec_g[...] = dot(fwd_ref[...], gate_s[...])

    def correlate(t, carry):
        at = pl.ds(pl.multiple_of(t * LANES, LANES), LANES)
        for c in range(chunks):
            re, im = slice(c * ROWS, c * ROWS + ROWS), slice(span + c * ROWS, span + c * ROWS + ROWS)
            mr, mi = spec_m[re, at], spec_m[im, at]
            gr, gi = spec_g[re, at], spec_g[im, at]
            prod_s[0, re, at] = (gr * mr + gi * mi).astype(BF16)
            prod_s[0, im, at] = (gi * mr - gr * mi).astype(BF16)
        return carry

    lax.fori_loop(0, n * chans // LANES, correlate, 0)
    both = dot(inv_s[span:, :], prod_s[0])
    sums = both[:NODES] + both[NODES:]
    for d in range(n):
        fgn_stage[d] = sums[:, d * chans : (d + 1) * chans]

    def send_correlation(r, carry):
        d = lax.rem(me + r, n)
        to_ctx(fgn_stage.at[d], fgn_recv.at[me], fgn_send.at[d], fgn_sem.at[me], d).start()
        return carry

    lax.fori_loop(1, n, send_correlation, 0)

    def take_filter(r, carry):
        d = lax.rem(me + r, n)
        to_ctx(hn_stage, hn_recv.at[d], hn_send.at[d], hn_sem.at[d], d).wait()
        return carry

    lax.fori_loop(1, n, take_filter, 0)

    own = jnp.concatenate([hn_recv[d] for d in range(n)], axis=1)
    spec_h[...] = dot(resp_ref[...], jnp.concatenate([own, own], axis=0))

    take_others(pq_stage, pq_recv, pq_send, pq_sem)

    def weigh(buffer, rows, k, table, sums):
        return [total + buffer[i, rows + k : rows + k + 1, :] * table[k] for i, total in enumerate(sums)]

    def states(j, carry):
        for i in range(2):
            row_s[i] = pq_recv[2 * j + i].astype(F32)
        a_sums = [jnp.zeros((MODES, chans), F32) for _ in range(2)]
        r_sums = [jnp.zeros((MODES, chans), F32) for _ in range(2)]
        for k in range(NODES):
            a_sums = weigh(row_s, 0, k, ep_s, a_sums)
            r_sums = weigh(row_s, NODES, k, e_s, r_sums)
        for i in range(2):
            a_s[2 * j + i] = a_sums[i]
            r_s[2 * j + i] = r_sums[i]
        return carry

    lax.fori_loop(0, n // 2, states, 0)
    step = jnp.exp(-decay_ref[...] * float(span))

    def recur(i, carry):
        forward_state, backward_state = carry
        s_s[i] = forward_state
        u_s[n - 1 - i] = backward_state
        return step * forward_state + a_s[i], step * backward_state + r_s[n - 1 - i]

    nothing = jnp.zeros((MODES, chans), F32)
    lax.fori_loop(0, n, recur, (nothing, nothing))

    def respond(r, carry):
        pair_of = [2 * across(me // 2, r, n // 2) + i if n > 2 else i for i in range(2)]
        y_sums = [jnp.zeros((NODES, chans), F32) for _ in range(2)]
        z_sums = [jnp.zeros((NODES, chans), F32) for _ in range(2)]
        for m in range(MODES):
            y_sums = [total + s_s[d, m : m + 1, :] * gt_s[m] for d, total in zip(pair_of, y_sums)]
            z_sums = [total + u_s[d, m : m + 1, :] * gr_s[m] for d, total in zip(pair_of, z_sums)]
        for i in range(2):
            yz_stage[pair_of[i]] = jnp.concatenate([y_sums[i], z_sums[i]], axis=0).astype(BF16)
        for d in pair_of:

            @pl.when(d != me)
            def _():
                to_ctx(yz_stage.at[d], yz_recv.at[me], yz_send.at[d], yz_sem.at[me], d).start()

        return carry

    lax.fori_loop(1, n // 2 + 1, respond, 0)
    yz_recv[me] = yz_stage[me]

    def inside(t, carry):
        at = pl.ds(pl.multiple_of(t * LANES, LANES), LANES)
        for c in range(chunks):
            re, im = slice(c * ROWS, c * ROWS + ROWS), slice(span + c * ROWS, span + c * ROWS + ROWS)
            hr, hi = spec_h[re, at], spec_h[im, at]
            mr, mi = spec_m[re, at], spec_m[im, at]
            gr, gi = spec_g[re, at], spec_g[im, at]
            prod_s[0, re, at] = (hr * mr - hi * mi).astype(BF16)
            prod_s[0, im, at] = (hr * mi + hi * mr).astype(BF16)
            prod_s[1, re, at] = (hr * gr + hi * gi).astype(BF16)
            prod_s[1, im, at] = (hr * gi - hi * gr).astype(BF16)
        return carry

    lax.fori_loop(0, n * chans // LANES, inside, 0)
    conv_s[...] = dot(inv_s[:span, :], prod_s[0])
    back_s[...] = dot(inv_s[:span, :], prod_s[1])

    def lags(j, carry):
        for i in range(2):
            sums = pq_recv[2 * j + i].astype(F32)
            row_s[i, :NODES] = sums[:NODES] * (float(span) - node_ref[...])
            row_s[i, NODES:] = sums[NODES:] * node_ref[...]
        a_sums = [jnp.zeros((MODES, chans), F32) for _ in range(2)]
        r_sums = [jnp.zeros((MODES, chans), F32) for _ in range(2)]
        for k in range(NODES):
            a_sums = weigh(row_s, 0, k, ep_s, a_sums)
            r_sums = weigh(row_s, NODES, k, e_s, r_sums)
        for i in range(2):
            al_s[2 * j + i] = a_sums[i]
            rl_s[2 * j + i] = r_sums[i]
        return carry

    lax.fori_loop(0, n // 2, lags, 0)

    def pair(i, carry):
        lag_state, exp_sum, lag_sum = carry
        state, reach = s_s[i], r_s[i]
        exp_sum = exp_sum + reach * state
        lag_sum = lag_sum + rl_s[i] * state + reach * lag_state
        return step * (lag_state + float(span) * state) + al_s[i], exp_sum, lag_sum

    _, exp_sum, lag_sum = lax.fori_loop(0, n, pair, (nothing, nothing, nothing))
    take_others(fgn_stage, fgn_recv, fgn_send, fgn_sem)
    fgn_recv[me] = fgn_stage[me]
    near_sum = fgn_recv[0]
    for d in range(1, n):
        near_sum = near_sum + fgn_recv[d]
    row_s[0, :NODES] = near_sum
    row_s[0, NODES:] = near_sum * node_ref[...]
    for k in range(NODES):
        exp_sum = exp_sum + row_s[0, k : k + 1, :] * e_s[k]
        lag_sum = lag_sum + row_s[0, NODES + k : NODES + k + 1, :] * e_s[k]
    mode_grads = (
        par_s[1] * exp_sum,
        res_ref[...] * jnp.exp(-2.0 * decay_ref[...]) / par_s[1] * exp_sum - par_s[0] * lag_sum,
    )

    def tile_of(index):
        row, lane = index // (chans // LANES), index % (chans // LANES)
        per = GRADS // 8 * (chans // LANES) // near
        return row // 2, row % 2 * 8, lane * LANES, index // per, index % per * 8

    tiles = range(GRADS // 8 * (chans // LANES))
    for index in tiles:
        which, row, lane, slot, place = tile_of(index)
        mode_stage[slot, place : place + 8, :] = mode_grads[which][row : row + 8, lane : lane + LANES]

    def send_near(source, target, send, recv):
        def one(r, carry):
            p = lax.rem(mine + r, near)
            to_dp(source(p), target.at[mine], send.at[p], recv.at[mine], block * near + p).start()
            return carry

        lax.fori_loop(1, near, one, 0)

    def take_near(target, send, recv):
        def one(r, carry):
            p = lax.rem(mine + r, near)
            to_dp(target.at[p], target.at[p], send.at[p], recv.at[p], block * near + p).wait()
            return carry

        lax.fori_loop(1, near, one, 0)

    def send_far(target, send, recv):
        def one(r, carry):
            b = lax.rem(block + r, groups)
            to_dp(target.at[block], target.at[block], send.at[b], recv.at[block], b * near + mine).start()
            return carry

        lax.fori_loop(1, groups, one, 0)

    def take_far(target, send, recv):
        def one(r, carry):
            b = lax.rem(block + r, groups)
            to_dp(target.at[b], target.at[b], send.at[b], recv.at[b], b * near + mine).wait()
            return carry

        lax.fori_loop(1, groups, one, 0)

    def sum_of(buffer):
        total = buffer[0]
        for p in range(1, buffer.shape[0]):
            total = total + buffer[p]
        return total

    send_near(lambda p: mode_stage.at[p], mode_one, mo_send, mo_sem)
    mode_one[mine] = mode_stage[mine]

    take_others(yz_stage, yz_recv, yz_send, yz_sem)
    for which in range(2):
        rows = slice(which * NODES, (which + 1) * NODES)
        node = jnp.concatenate([yz_recv[d, rows] for d in range(n)], axis=1)
        far_s[which] = dot(spread_ref[...], jnp.concatenate([node, node], axis=0))

    def finish(r, carry):
        first = first_of(r)

        def gradients(g, carry):
            for t in range(chans // LANES):
                some = pl.ds(pl.multiple_of(g * chans + t * LANES, LANES), LANES)
                at = pl.ds(pl.multiple_of((first + g) * chans + t * LANES, LANES), LANES)
                totals = [jnp.zeros((8, LANES), F32) for _ in range(9)]
                for c in range(chunks):
                    low = c * ROWS
                    rows = slice(low, low + ROWS)
                    conv = (conv_s[rows, at] + far_s[0, rows, at]).astype(BF16).astype(F32)
                    back = (back_s[rows, at] + far_s[1, rows, at]).astype(BF16).astype(F32)
                    conv_s[rows, at] = conv
                    back_s[rows, at] = back
                    grads = [
                        cot_ref[rows, at].astype(F32) * conv,
                        back * value_s[rows, at],
                        back * key_s[rows, at],
                    ]
                    lag = [xs[8 + low - j : 8 + low - j + ROWS, at] for j in range(3)]
                    for s in range(3):
                        fg_s[s * span + low : s * span + low + ROWS, some] = grads[s].astype(BF16)
                        for j in range(3):
                            part = grads[s] * lag[j]
                            totals[3 * s + j] = totals[3 * s + j] + (part[:8] + part[8:])
                for i in range(9):
                    sums_s[g, 12 + i : 13 + i, t * LANES : (t + 1) * LANES] = jnp.sum(totals[i], axis=0, keepdims=True)
            return carry

        lax.fori_loop(0, wide, gradients, 0)
        letter_sums = dot(hot_t[...], fg_s[...])
        for g in range(wide):
            sums_s[g, :12, :] = letter_sums[:12, g * chans : (g + 1) * chans]
            sums_s[g, 21:, :] = jnp.zeros((PIECE - 21, chans), F32)
            piece_stage[first + g] = packed(sums_s[g])
        send_others(first, piece_stage, piece_recv, piece_send, piece_sem)
        return carry

    lax.fori_loop(1, sets + 1, finish, 0)

    take_near(mode_one, mo_send, mo_sem)
    mode_two[block] = sum_of(mode_one)
    send_far(mode_two, mt_send, mt_sem)

    take_others(piece_stage, piece_recv, piece_send, piece_sem)
    piece_recv[me] = piece_stage[me]
    piece = piece_recv[0].astype(F32)
    for d in range(1, n):
        piece = piece + piece_recv[d].astype(F32)
    tap_far[block] = unpacked(piece)
    send_far(tap_far, tf_send, tf_sem)

    w_s[0, span : span + 8, :] = jnp.zeros((8, chans), F32)
    w_s[1, span : span + 8, :] = jnp.zeros((8, chans), F32)

    def input_gradient(d, carry):
        for t in range(chans // LANES):
            some = slice(t * LANES, (t + 1) * LANES)
            at = pl.ds(pl.multiple_of(d * chans + t * LANES, LANES), LANES)
            tap = [tap_s[i : i + 1, at] for i in range(9)]
            for c in reversed(range(chunks)):
                low = c * ROWS
                rows = slice(low, low + ROWS)
                back = back_s[rows, at]
                grads = [cot_ref[rows, at].astype(F32) * conv_s[rows, at], back * value_s[rows, at], back * key_s[rows, at]]
                ahead_by = [tap[j] * grads[0] + tap[3 + j] * grads[1] + tap[6 + j] * grads[2] for j in range(3)]
                w_s[0, rows, some] = ahead_by[1]
                w_s[1, rows, some] = ahead_by[2]
                part = (
                    ahead_by[0]
                    + w_s[0, low + 1 : low + 1 + ROWS, some]
                    + w_s[1, low + 2 : low + 2 + ROWS, some]
                )
                if c < chunks - 1:
                    grad_ref[rows, at] = part.astype(BF16)
                else:
                    tail_s[:, at] = part
            edge_stage[0:1, at] = w_s[1, 0:1, some]
            edge_stage[1:2, at] = w_s[0, 0:1, some] + w_s[1, 1:2, some]
        return carry

    lax.fori_loop(0, n, input_gradient, 0)
    edge = to_ctx(edge_stage, edge_recv, edge_sem.at[2], edge_sem.at[3], behind)
    edge.start()
    body = pl.ds(0, span - ROWS)
    main = pltpu.make_async_copy(grad_ref.at[body, :], grad_hbm.at[body, :], out_sem.at[0])
    main.start()

    edge.wait()
    tail_s[ROWS - 2 :, :] = tail_s[ROWS - 2 :, :] + jnp.where(me < n - 1, edge_recv[...], 0.0)
    grad_ref[span - ROWS :, :] = tail_s[...].astype(BF16)
    last = pl.ds(span - ROWS, ROWS)
    tail = pltpu.make_async_copy(grad_ref.at[last, :], grad_hbm.at[last, :], out_sem.at[1])
    tail.start()

    take_far(mode_two, mt_send, mt_sem)
    mode_three[mine] = sum_of(mode_two)
    send_near(lambda p: mode_three.at[mine], mode_three, mh_send, mh_sem)
    take_far(tap_far, tf_send, tf_sem)
    tap_near[mine] = packed(sum_of(tap_far))
    for copy, _ in around:
        copy().start()
    main.wait()
    tail.wait()
    take_near(mode_three, mh_send, mh_sem)
    for index in tiles:
        which, row, lane, slot, place = tile_of(index)
        row = PIECE + which * MODES + row
        total_ref[row : row + 8, lane : lane + LANES] = mode_three[slot, place : place + 8, :]
    for _, copy in around:
        copy().wait()
    total = tap_near[0].astype(F32)
    for p in range(1, near):
        total = total + tap_near[p].astype(F32)
    total_ref[:PIECE, :] = unpacked(total)


def hand_out(total_ref, grad_ref, grad_out, taps_out, table_out, res_out, decay_out):
    grad_out[...] = grad_ref[...]
    for s in range(3):
        table_out[s] = total_ref[4 * s : 4 * s + 4, :]
        taps_out[s] = total_ref[12 + 3 * s : 15 + 3 * s, :]
    res_out[...] = total_ref[PIECE : PIECE + MODES, :]
    decay_out[...] = total_ref[PIECE + MODES :, :]


def shards(n, near, groups, inputs, letters, letter_table, short_taps, residues, decay_rate, cotangent):
    span, width = inputs.shape[1:]
    chans = width // n
    wide = 4 if n % 8 == 0 else 2
    fixed = tables(span)
    nodes = fixed["nodes"]
    node_cols = np.broadcast_to(nodes[:, None], (NODES, chans)).astype(np.float32)
    vmem = pl.BlockSpec(memory_space=pltpu.VMEM)
    anywhere = pl.BlockSpec(memory_space=pl.ANY)
    dma = pltpu.SemaphoreType.DMA
    operands = [inputs[0], letters, letter_table, short_taps, residues.T, decay_rate.T, cotangent[0]] + [
        jnp.asarray(fixed[name]) for name in ("forward", "moments", "inverse", "spread", "response")
    ] + [jnp.asarray(node_cols)]
    several = wide * chans
    share = GRADS * chans // LANES // near
    scratch = [pltpu.VMEM(value.shape, value.dtype) for value in operands] + [
        pltpu.VMEM((ROWS, width), BF16),
        pltpu.VMEM((span + 2 * NODES, 2 * span), BF16),
        pltpu.VMEM((span, width), BF16),
        pltpu.VMEM((span + 8, width), F32),
        pltpu.VMEM((span, width), F32),
        pltpu.VMEM((span, width), F32),
        pltpu.VMEM((span, width), BF16),
        pltpu.VMEM((span, width), BF16),
        pltpu.VMEM((span, width), F32),
        pltpu.VMEM((span, width), F32),
        pltpu.VMEM((span, LANES), F32),
        pltpu.VMEM((ROWS, 3 * span), BF16),
        pltpu.VMEM((ROWS, width), F32),
        pltpu.VMEM((ROWS, width), F32),
        pltpu.VMEM((2 * span, width), F32),
        pltpu.VMEM((2 * span, width), F32),
        pltpu.VMEM((2 * span, width), F32),
        pltpu.VMEM((2, 2 * span, width), BF16),
        pltpu.VMEM((2, span, width), F32),
        pltpu.VMEM((3 * span, several), BF16),
        pltpu.VMEM((wide, PIECE, chans), F32),
        pltpu.VMEM((2, span + 8, chans), F32),
        pltpu.VMEM((ROWS, width), F32),
    ] + [pltpu.VMEM((NODES, MODES, chans), F32)] * 4 + [pltpu.VMEM((n, MODES, chans), F32)] * 6 + [
        pltpu.VMEM((2, 2 * NODES, chans), F32),
        pltpu.VMEM((2, MODES, chans), F32),
    ] + [pltpu.VMEM((2, width), F32)] * 4 + [
        pltpu.VMEM((NODES, chans), BF16),
        pltpu.VMEM((n, NODES, chans), BF16),
        pltpu.VMEM((n, 2 * NODES, chans), BF16),
        pltpu.VMEM((n, 2 * NODES, chans), BF16),
        pltpu.VMEM((n, NODES, chans), F32),
        pltpu.VMEM((n, NODES, chans), F32),
        pltpu.VMEM((n, 2 * NODES, chans), BF16),
        pltpu.VMEM((n, 2 * NODES, chans), BF16),
        pltpu.VMEM((n, 16, chans * 3 // 2), BF16),
        pltpu.VMEM((n, 16, chans * 3 // 2), BF16),
        pltpu.VMEM((near, share, LANES), F32),
        pltpu.VMEM((near, share, LANES), F32),
        pltpu.VMEM((groups, share, LANES), F32),
        pltpu.VMEM((near, share, LANES), F32),
        pltpu.VMEM((near, 16, chans * 3 // 2), BF16),
        pltpu.VMEM((groups, PIECE, chans), F32),
        dma((len(operands) + 1,)),
        dma((2,)),
        dma((4,)),
    ] + [dma((n,))] * 10 + ([dma((near,))] * 2 + [dma((groups,))] * 2 + [dma((near,))] * 2) + [dma((near,))] * 2 + [dma((groups,))] * 2
    grad, total = pl.pallas_call(
        functools.partial(kernel, n, near, groups, wide, span, chans, nodes),
        out_shape=(
            jax.ShapeDtypeStruct((span, width), BF16),
            jax.ShapeDtypeStruct((PIECE + GRADS, chans), F32),
        ),
        in_specs=[anywhere] * len(operands),
        out_specs=(anywhere, vmem),
        scratch_shapes=scratch,
        compiler_params=pltpu.CompilerParams(
            collective_id=0, has_side_effects=True, vmem_limit_bytes=56 * 1024 * 1024
        ),
    )(*operands)
    grad, taps_grad, table_grad, residue_grad, decay_grad = pl.pallas_call(
        hand_out,
        out_shape=(
            jax.ShapeDtypeStruct((span, width), BF16),
            jax.ShapeDtypeStruct((3, 3, chans), F32),
            jax.ShapeDtypeStruct((3, 4, chans), F32),
            jax.ShapeDtypeStruct((MODES, chans), F32),
            jax.ShapeDtypeStruct((MODES, chans), F32),
        ),
        in_specs=[vmem] * 2,
        out_specs=(vmem,) * 5,
        compiler_params=pltpu.CompilerParams(vmem_limit_bytes=56 * 1024 * 1024),
    )(total, grad)
    return grad[None], taps_grad, table_grad, residue_grad.T, decay_grad.T


def solution(mesh):
    n, sequences = mesh.shape["ctx"], mesh.shape["dp"]
    near = max(k for k in (1, 2, 4, 8) if sequences % k == 0 and k * k <= 2 * sequences)
    in_specs = (
        P("dp", "ctx", None),
        P("dp", "ctx"),
        P(),
        P(),
        P("ctx", None),
        P("ctx", None),
        P("dp", "ctx", None),
    )
    out_specs = (
        P("dp", "ctx", None),
        P(None, None, "ctx"),
        P(None, None, "ctx"),
        P("ctx", None),
        P("ctx", None),
    )
    body = functools.partial(shards, n, near, sequences // near)
    return jax.shard_map(body, mesh=mesh, in_specs=in_specs, out_specs=out_specs, check_vma=False)
```

```python
import functools

import jax
import jax.numpy as jnp
import numpy as np
from jax import lax
from jax.experimental import pallas as pl
from jax.experimental.pallas import tpu as pltpu
from jax.sharding import PartitionSpec as P

MESH = pl.DeviceIdType.MESH
F32 = jnp.float32
BF16 = jnp.bfloat16
NODES = 16
MODES = 16
ROWS = 16
PIECE = 24
GRADS = 2 * MODES
LANES = 128


def split(values):
    high = values.astype(jnp.bfloat16)
    low = (values - high.astype(np.float64)).astype(jnp.bfloat16)
    return high, low


def tables(span):
    half = span / 2
    centre = (span - 1) / 2
    angles = np.pi * (2 * np.arange(NODES) + 1) / (2 * NODES)
    nodes = centre + half * np.cos(angles)
    places = np.arange(span)
    interp = np.ones((span, NODES))
    for k in range(NODES):
        for other in range(NODES):
            if other != k:
                interp[:, k] *= (places - nodes[other]) / (nodes[k] - nodes[other])
    theta = 2 * np.pi * (np.arange(span) + 0.5) / (2 * span)
    phase = theta[:, None] * places[None, :]
    forward = np.concatenate([np.cos(phase), -np.sin(phase)], axis=0)
    inverse = np.concatenate([np.cos(phase.T), -np.sin(phase.T)], axis=1) / span
    l_hi, l_lo = split(interp)
    w_hi, w_lo = split(forward @ interp)
    m_hi, m_lo = split(interp.T @ inverse)
    return dict(
        nodes=nodes,
        forward=forward.astype(jnp.bfloat16),
        moments=np.concatenate([l_hi.T, l_lo.T], axis=0),
        inverse=np.concatenate([inverse, m_hi.astype(np.float64), m_lo.astype(np.float64)], axis=0).astype(np.float32),
        spread=np.concatenate([l_hi, l_lo], axis=1),
        response=np.concatenate([w_hi, w_lo], axis=1),
    )


def packed(rows):
    half = rows.shape[1] // 2
    return jnp.concatenate(
        [rows[:16], jnp.concatenate([rows[16:, :half], rows[16:, half:]], axis=0)], axis=1
    ).astype(BF16)


def unpacked(block):
    wide = block.shape[1] // 3 * 2
    block = block.astype(F32)
    return jnp.concatenate(
        [block[:, :wide], jnp.concatenate([block[:8, wide:], block[8:, wide:]], axis=1)], axis=0
    )


def dot(left, right):
    return jnp.dot(left, right, preferred_element_type=F32)


def kernel(n, near, groups, wide, span, chans, nodes, *refs):
    (
        x_hbm, letters_hbm, table_hbm, taps_hbm, res_hbm, decay_hbm, cot_hbm,
        fwd_hbm, mom_hbm, inv_hbm, spread_hbm, resp_hbm, node_hbm,
        grad_hbm, total_ref,
        x_ref, letters_ref, table_ref, taps_ref, res_ref, decay_ref, cot_ref,
        fwd_ref, mom_ref, inv_ref, spread_ref, resp_ref, node_ref,
        x_last, inv_s, grad_ref, xs, key_s, value_s, mix_s, gate_s, conv_s, back_s,
        code_s, hot_t, tab_s, tap_s, spec_m, spec_g, spec_h, prod_s, far_s, fg_s, sums_s, w_s, tail_s,
        e_s, ep_s, gt_s, gr_s, a_s, r_s, s_s, u_s, al_s, rl_s, row_s, par_s,
        halo_stage, halo_recv, edge_stage, edge_recv,
        hn_stage, hn_recv, pq_stage, pq_recv, fgn_stage, fgn_recv,
        yz_stage, yz_recv, piece_stage, piece_recv,
        mode_stage, mode_one, mode_two, mode_three, tap_near, tap_far,
        in_sem, out_sem, edge_sem,
        hn_send, hn_sem, pq_send, pq_sem, fgn_send, fgn_sem, yz_send, yz_sem, piece_send, piece_sem,
        mo_send, mo_sem, mt_send, mt_sem, mh_send, mh_sem, tn_send, tn_sem, tf_send, tf_sem,
    ) = refs
    me = lax.axis_index("ctx")
    seq = lax.axis_index("dp")
    mine, block = lax.rem(seq, near), seq // near
    ahead, behind = lax.rem(me + 1, n), lax.rem(me + n - 1, n)
    sets = n // wide
    width = wide * chans
    chunks = span // ROWS

    def lanes(d):
        return pl.ds(pl.multiple_of(d * chans, chans), chans)

    def set_lanes(first):
        return pl.ds(pl.multiple_of(first * chans, width), width)

    def across(position, r, count):
        side_size = count // 2
        side = lax.rem(position // side_size + 1 - (r - 1) // side_size, 2)
        return side * side_size + lax.rem(position + r, side_size)

    def first_of(r):
        return across(me // wide, r, sets) * wide if sets > 1 else 0

    def to_ctx(source, target, send, recv, d):
        return pltpu.make_async_remote_copy(
            src_ref=source, dst_ref=target, send_sem=send, recv_sem=recv,
            device_id=(seq, d), device_id_type=MESH,
        )

    def to_dp(source, target, send, recv, p):
        return pltpu.make_async_remote_copy(
            src_ref=source, dst_ref=target, send_sem=send, recv_sem=recv,
            device_id=(p, me), device_id_type=MESH,
        )

    def send_others(first, stage, recv_buffer, send, recv):
        for g in range(wide):
            d = first + g

            @pl.when(d != me)
            def _():
                to_ctx(stage.at[d], recv_buffer.at[me], send.at[d], recv.at[me], d).start()

    def take_others(stage, recv_buffer, send, recv):
        def take(r, carry):
            d = lax.rem(me + r, n)
            to_ctx(stage.at[d], recv_buffer.at[d], send.at[d], recv.at[d], d).wait()
            return carry

        lax.fori_loop(1, n, take, 0)

    steps = near // 2
    along, side = seq // 2, lax.rem(seq, 2)
    places = near * groups // 2
    offsets = range(-((steps - 1) // 2), steps - (steps - 1) // 2)

    def at_offset(offset, other):
        return lax.rem(along + offset + places, places) * 2 + lax.rem(side + other, 2)

    def around_copies(index, offset, other):
        def outward():
            return to_dp(tap_near.at[mine], tap_near.at[mine], tn_send.at[index], tn_sem.at[mine], at_offset(-offset, other))

        def inward():
            slot = lax.rem(at_offset(offset, other), near)
            return to_dp(tap_near.at[slot], tap_near.at[slot], tn_send.at[index], tn_sem.at[slot], at_offset(offset, other))

        return outward, inward

    around = [
        around_copies(index, offset, other)
        for index, (offset, other) in enumerate((o, s) for o in sorted(offsets, key=abs, reverse=True) for s in (1, 0) if (o, s) != (0, 0))
    ]

    barrier = pltpu.get_barrier_semaphore()

    loads = [
        pltpu.make_async_copy(source, target, in_sem.at[i])
        for i, (source, target) in enumerate([
            (x_hbm.at[pl.ds(span - ROWS, ROWS), :], x_last),
            (res_hbm, res_ref), (decay_hbm, decay_ref), (node_hbm, node_ref), (x_hbm, x_ref),
            (letters_hbm, letters_ref), (table_hbm, table_ref), (taps_hbm, taps_ref), (cot_hbm, cot_ref),
            (mom_hbm, mom_ref),
            (fwd_hbm, fwd_ref), (inv_hbm, inv_ref), (resp_hbm, resp_ref), (spread_hbm, spread_ref),
        ])
    ]
    for load in loads:
        load.start()

    def greet_ctx(r, carry):
        pl.semaphore_signal(barrier, inc=1, device_id=(seq, lax.rem(me + r, n)), device_id_type=MESH)
        return carry

    def greet_near(r, carry):
        peer = block * near + lax.rem(mine + r, near)
        pl.semaphore_signal(barrier, inc=1, device_id=(peer, me), device_id_type=MESH)
        return carry

    def greet_far(r, carry):
        peer = lax.rem(block + r, groups) * near + mine
        pl.semaphore_signal(barrier, inc=1, device_id=(peer, me), device_id_type=MESH)
        return carry

    lax.fori_loop(1, n, greet_ctx, 0)
    lax.fori_loop(1, near, greet_near, 0)
    lax.fori_loop(1, groups, greet_far, 0)
    greeted = [(o, s) for o in sorted(set(offsets) | {-o for o in offsets}) for s in range(2) if (o, s) != (0, 0)]
    for offset, other in greeted:
        pl.semaphore_signal(barrier, inc=1, device_id=(at_offset(offset, other), me), device_id_type=MESH)

    for load in loads[1:4]:
        load.wait()
    rate, weight = decay_ref[...], res_ref[...]
    twice = 2.0 * rate
    series = 1.0 - twice * (1.0 / 7.0)
    for term in (6.0, 5.0, 4.0, 3.0, 2.0):
        series = 1.0 - twice * (1.0 / term) * series
    scale = jnp.sqrt(twice * series)
    gain = weight * scale
    par_s[0] = gain
    par_s[1] = scale
    node_col = node_ref[...]
    own_filter = jnp.zeros((NODES, chans), F32)
    for m in range(MODES):
        wave = par_s[0, m : m + 1, :] * jnp.exp(-decay_ref[m : m + 1, :] * node_col)
        gt_s[m] = wave
        own_filter = own_filter + wave
    hn_stage[...] = own_filter.astype(BF16)
    hn_recv[me] = own_filter.astype(BF16)

    for m in range(MODES):
        gr_s[m] = par_s[0, m : m + 1, :] * jnp.exp(-decay_ref[m : m + 1, :] * (float(span) - node_col))
    for k in range(NODES):
        e_s[k] = jnp.exp(-rate * float(nodes[k]))
        ep_s[k] = jnp.exp(-rate * float(span - nodes[k]))

    loads[0].wait()
    halo_stage[...] = x_last[...].astype(F32)[ROWS - 2 :, :]
    pl.semaphore_wait(barrier, (n - 1) + (near - 1) + (groups - 1) + len(greeted))
    halo = to_ctx(halo_stage, halo_recv, edge_sem.at[0], edge_sem.at[1], ahead)
    halo.start()

    def send_filter(r, carry):
        d = lax.rem(me + r, n)
        to_ctx(hn_stage, hn_recv.at[me], hn_send.at[d], hn_sem.at[me], d).start()
        return carry

    lax.fori_loop(1, n, send_filter, 0)
    for load in loads[4:9]:
        load.wait()

    codes = jnp.concatenate([letters_ref[...] + 4 * s for s in range(3)], axis=1)
    hot_t[...] = (lax.broadcasted_iota(jnp.int32, (ROWS, 3 * span), 0) == codes).astype(F32).astype(BF16)
    code_s[...] = jnp.transpose(jnp.broadcast_to(letters_ref[...].astype(F32), (LANES, span)))

    def products(at, which):
        tap = [tap_s[i : i + 1, at] for i in range(9)]
        tab = [tab_s[i : i + 1, at] for i in range(12)]
        for c in which:
            low = c * ROWS
            rows = slice(low, low + ROWS)
            code = code_s[rows, :]
            is_one, is_two, is_three = code == 1.0, code == 2.0, code == 3.0
            lag = [xs[8 + low - j : 8 + low - j + ROWS, at] for j in range(3)]
            stream = []
            for s in range(3):
                part = jnp.where(
                    is_one,
                    tab[4 * s + 1],
                    jnp.where(is_two, tab[4 * s + 2], jnp.where(is_three, tab[4 * s + 3], tab[4 * s])),
                )
                for j in range(3):
                    part = part + tap[3 * s + j] * lag[j]
                stream.append(part)
            key_s[rows, at] = stream[1]
            value_s[rows, at] = stream[2]
            mix_s[rows, at] = (stream[1] * stream[2]).astype(BF16)
            gate_s[rows, at] = (cot_ref[rows, at].astype(F32) * stream[0]).astype(BF16)

    def late_rows(g, carry):
        at = lanes(g)
        xs[8:, at] = x_ref[:, at].astype(F32)
        for s in range(3):
            tap_s[3 * s : 3 * s + 3, at] = taps_ref[s, :, at].astype(F32)
            tab_s[4 * s : 4 * s + 4, at] = table_ref[s, :, at].astype(F32)
        for t in range(chans // LANES):
            products(pl.ds(pl.multiple_of(g * chans + t * LANES, LANES), LANES), range(1, chunks))
        return carry

    lax.fori_loop(0, n, late_rows, 0)
    loads[9].wait()
    halo.wait()
    xs[6:8, :] = jnp.where(me > 0, halo_recv[...], 0.0)

    def node_sums(r, carry):
        first = first_of(r)
        for t in range(width // LANES):
            products(pl.ds(pl.multiple_of(first * chans + t * LANES, LANES), LANES), range(1))
        at = set_lanes(first)
        p_sum = dot(mom_ref[...], mix_s[:, at])
        q_sum = dot(mom_ref[...], gate_s[:, at])
        sums = jnp.concatenate([p_sum[:NODES] + p_sum[NODES:], q_sum[:NODES] + q_sum[NODES:]], axis=0).astype(BF16)
        for g in range(wide):
            pq_stage[first + g] = sums[:, g * chans : (g + 1) * chans]
        send_others(first, pq_stage, pq_recv, pq_send, pq_sem)
        return carry

    lax.fori_loop(1, sets + 1, node_sums, 0)
    pq_recv[me] = pq_stage[me]

    for load in loads[10:]:
        load.wait()
    inv_s[...] = inv_ref[...].astype(BF16)

    spec_m[...] = dot(fwd_ref[...], mix_s[...])
    spec_g[...] = dot(fwd_ref[...], gate_s[...])

    def correlate(t, carry):
        at = pl.ds(pl.multiple_of(t * LANES, LANES), LANES)
        for c in range(chunks):
            re, im = slice(c * ROWS, c * ROWS + ROWS), slice(span + c * ROWS, span + c * ROWS + ROWS)
            mr, mi = spec_m[re, at], spec_m[im, at]
            gr, gi = spec_g[re, at], spec_g[im, at]
            prod_s[0, re, at] = (gr * mr + gi * mi).astype(BF16)
            prod_s[0, im, at] = (gi * mr - gr * mi).astype(BF16)
        return carry

    lax.fori_loop(0, n * chans // LANES, correlate, 0)
    both = dot(inv_s[span:, :], prod_s[0])
    sums = both[:NODES] + both[NODES:]
    for d in range(n):
        fgn_stage[d] = sums[:, d * chans : (d + 1) * chans]

    def send_correlation(r, carry):
        d = lax.rem(me + r, n)
        to_ctx(fgn_stage.at[d], fgn_recv.at[me], fgn_send.at[d], fgn_sem.at[me], d).start()
        return carry

    lax.fori_loop(1, n, send_correlation, 0)

    def take_filter(r, carry):
        d = lax.rem(me + r, n)
        to_ctx(hn_stage, hn_recv.at[d], hn_send.at[d], hn_sem.at[d], d).wait()
        return carry

    lax.fori_loop(1, n, take_filter, 0)

    own = jnp.concatenate([hn_recv[d] for d in range(n)], axis=1)
    spec_h[...] = dot(resp_ref[...], jnp.concatenate([own, own], axis=0))

    take_others(pq_stage, pq_recv, pq_send, pq_sem)

    def weigh(buffer, rows, k, table, sums):
        return [total + buffer[i, rows + k : rows + k + 1, :] * table[k] for i, total in enumerate(sums)]

    def states(j, carry):
        for i in range(2):
            row_s[i] = pq_recv[2 * j + i].astype(F32)
        a_sums = [jnp.zeros((MODES, chans), F32) for _ in range(2)]
        r_sums = [jnp.zeros((MODES, chans), F32) for _ in range(2)]
        for k in range(NODES):
            a_sums = weigh(row_s, 0, k, ep_s, a_sums)
            r_sums = weigh(row_s, NODES, k, e_s, r_sums)
        for i in range(2):
            a_s[2 * j + i] = a_sums[i]
            r_s[2 * j + i] = r_sums[i]
        return carry

    lax.fori_loop(0, n // 2, states, 0)
    step = jnp.exp(-decay_ref[...] * float(span))

    def recur(i, carry):
        forward_state, backward_state = carry
        s_s[i] = forward_state
        u_s[n - 1 - i] = backward_state
        return step * forward_state + a_s[i], step * backward_state + r_s[n - 1 - i]

    nothing = jnp.zeros((MODES, chans), F32)
    lax.fori_loop(0, n, recur, (nothing, nothing))

    def respond(r, carry):
        pair_of = [2 * across(me // 2, r, n // 2) + i if n > 2 else i for i in range(2)]
        y_sums = [jnp.zeros((NODES, chans), F32) for _ in range(2)]
        z_sums = [jnp.zeros((NODES, chans), F32) for _ in range(2)]
        for m in range(MODES):
            y_sums = [total + s_s[d, m : m + 1, :] * gt_s[m] for d, total in zip(pair_of, y_sums)]
            z_sums = [total + u_s[d, m : m + 1, :] * gr_s[m] for d, total in zip(pair_of, z_sums)]
        for i in range(2):
            yz_stage[pair_of[i]] = jnp.concatenate([y_sums[i], z_sums[i]], axis=0).astype(BF16)
        for d in pair_of:

            @pl.when(d != me)
            def _():
                to_ctx(yz_stage.at[d], yz_recv.at[me], yz_send.at[d], yz_sem.at[me], d).start()

        return carry

    lax.fori_loop(1, n // 2 + 1, respond, 0)
    yz_recv[me] = yz_stage[me]

    def inside(t, carry):
        at = pl.ds(pl.multiple_of(t * LANES, LANES), LANES)
        for c in range(chunks):
            re, im = slice(c * ROWS, c * ROWS + ROWS), slice(span + c * ROWS, span + c * ROWS + ROWS)
            hr, hi = spec_h[re, at], spec_h[im, at]
            mr, mi = spec_m[re, at], spec_m[im, at]
            gr, gi = spec_g[re, at], spec_g[im, at]
            prod_s[0, re, at] = (hr * mr - hi * mi).astype(BF16)
            prod_s[0, im, at] = (hr * mi + hi * mr).astype(BF16)
            prod_s[1, re, at] = (hr * gr + hi * gi).astype(BF16)
            prod_s[1, im, at] = (hr * gi - hi * gr).astype(BF16)
        return carry

    lax.fori_loop(0, n * chans // LANES, inside, 0)
    conv_s[...] = dot(inv_s[:span, :], prod_s[0])
    back_s[...] = dot(inv_s[:span, :], prod_s[1])

    def lags(j, carry):
        for i in range(2):
            sums = pq_recv[2 * j + i].astype(F32)
            row_s[i, :NODES] = sums[:NODES] * (float(span) - node_ref[...])
            row_s[i, NODES:] = sums[NODES:] * node_ref[...]
        a_sums = [jnp.zeros((MODES, chans), F32) for _ in range(2)]
        r_sums = [jnp.zeros((MODES, chans), F32) for _ in range(2)]
        for k in range(NODES):
            a_sums = weigh(row_s, 0, k, ep_s, a_sums)
            r_sums = weigh(row_s, NODES, k, e_s, r_sums)
        for i in range(2):
            al_s[2 * j + i] = a_sums[i]
            rl_s[2 * j + i] = r_sums[i]
        return carry

    lax.fori_loop(0, n // 2, lags, 0)

    def pair(i, carry):
        lag_state, exp_sum, lag_sum = carry
        state, reach = s_s[i], r_s[i]
        exp_sum = exp_sum + reach * state
        lag_sum = lag_sum + rl_s[i] * state + reach * lag_state
        return step * (lag_state + float(span) * state) + al_s[i], exp_sum, lag_sum

    _, exp_sum, lag_sum = lax.fori_loop(0, n, pair, (nothing, nothing, nothing))
    take_others(fgn_stage, fgn_recv, fgn_send, fgn_sem)
    fgn_recv[me] = fgn_stage[me]
    near_sum = fgn_recv[0]
    for d in range(1, n):
        near_sum = near_sum + fgn_recv[d]
    row_s[0, :NODES] = near_sum
    row_s[0, NODES:] = near_sum * node_ref[...]
    for k in range(NODES):
        exp_sum = exp_sum + row_s[0, k : k + 1, :] * e_s[k]
        lag_sum = lag_sum + row_s[0, NODES + k : NODES + k + 1, :] * e_s[k]
    mode_grads = (
        par_s[1] * exp_sum,
        res_ref[...] * jnp.exp(-2.0 * decay_ref[...]) / par_s[1] * exp_sum - par_s[0] * lag_sum,
    )

    def tile_of(index):
        row, lane = index // (chans // LANES), index % (chans // LANES)
        per = GRADS // 8 * (chans // LANES) // near
        return row // 2, row % 2 * 8, lane * LANES, index // per, index % per * 8

    tiles = range(GRADS // 8 * (chans // LANES))
    for index in tiles:
        which, row, lane, slot, place = tile_of(index)
        mode_stage[slot, place : place + 8, :] = mode_grads[which][row : row + 8, lane : lane + LANES]

    def send_near(source, target, send, recv):
        def one(r, carry):
            p = lax.rem(mine + r, near)
            to_dp(source(p), target.at[mine], send.at[p], recv.at[mine], block * near + p).start()
            return carry

        lax.fori_loop(1, near, one, 0)

    def take_near(target, send, recv):
        def one(r, carry):
            p = lax.rem(mine + r, near)
            to_dp(target.at[p], target.at[p], send.at[p], recv.at[p], block * near + p).wait()
            return carry

        lax.fori_loop(1, near, one, 0)

    def send_far(target, send, recv):
        def one(r, carry):
            b = lax.rem(block + r, groups)
            to_dp(target.at[block], target.at[block], send.at[b], recv.at[block], b * near + mine).start()
            return carry

        lax.fori_loop(1, groups, one, 0)

    def take_far(target, send, recv):
        def one(r, carry):
            b = lax.rem(block + r, groups)
            to_dp(target.at[b], target.at[b], send.at[b], recv.at[b], b * near + mine).wait()
            return carry

        lax.fori_loop(1, groups, one, 0)

    def sum_of(buffer):
        total = buffer[0]
        for p in range(1, buffer.shape[0]):
            total = total + buffer[p]
        return total

    send_near(lambda p: mode_stage.at[p], mode_one, mo_send, mo_sem)
    mode_one[mine] = mode_stage[mine]

    take_others(yz_stage, yz_recv, yz_send, yz_sem)
    for which in range(2):
        rows = slice(which * NODES, (which + 1) * NODES)
        node = jnp.concatenate([yz_recv[d, rows] for d in range(n)], axis=1)
        far_s[which] = dot(spread_ref[...], jnp.concatenate([node, node], axis=0))

    def finish(r, carry):
        first = first_of(r)

        def gradients(g, carry):
            for t in range(chans // LANES):
                some = pl.ds(pl.multiple_of(g * chans + t * LANES, LANES), LANES)
                at = pl.ds(pl.multiple_of((first + g) * chans + t * LANES, LANES), LANES)
                totals = [jnp.zeros((8, LANES), F32) for _ in range(9)]
                for c in range(chunks):
                    low = c * ROWS
                    rows = slice(low, low + ROWS)
                    conv = (conv_s[rows, at] + far_s[0, rows, at]).astype(BF16).astype(F32)
                    back = (back_s[rows, at] + far_s[1, rows, at]).astype(BF16).astype(F32)
                    conv_s[rows, at] = conv
                    back_s[rows, at] = back
                    grads = [
                        cot_ref[rows, at].astype(F32) * conv,
                        back * value_s[rows, at],
                        back * key_s[rows, at],
                    ]
                    lag = [xs[8 + low - j : 8 + low - j + ROWS, at] for j in range(3)]
                    for s in range(3):
                        fg_s[s * span + low : s * span + low + ROWS, some] = grads[s].astype(BF16)
                        for j in range(3):
                            part = grads[s] * lag[j]
                            totals[3 * s + j] = totals[3 * s + j] + (part[:8] + part[8:])
                for i in range(9):
                    sums_s[g, 12 + i : 13 + i, t * LANES : (t + 1) * LANES] = jnp.sum(totals[i], axis=0, keepdims=True)
            return carry

        lax.fori_loop(0, wide, gradients, 0)
        letter_sums = dot(hot_t[...], fg_s[...])
        for g in range(wide):
            sums_s[g, :12, :] = letter_sums[:12, g * chans : (g + 1) * chans]
            sums_s[g, 21:, :] = jnp.zeros((PIECE - 21, chans), F32)
            piece_stage[first + g] = packed(sums_s[g])
        send_others(first, piece_stage, piece_recv, piece_send, piece_sem)
        return carry

    lax.fori_loop(1, sets + 1, finish, 0)

    take_near(mode_one, mo_send, mo_sem)
    mode_two[block] = sum_of(mode_one)
    send_far(mode_two, mt_send, mt_sem)

    take_others(piece_stage, piece_recv, piece_send, piece_sem)
    piece_recv[me] = piece_stage[me]
    piece = piece_recv[0].astype(F32)
    for d in range(1, n):
        piece = piece + piece_recv[d].astype(F32)
    tap_far[block] = unpacked(piece)
    send_far(tap_far, tf_send, tf_sem)

    w_s[0, span : span + 8, :] = jnp.zeros((8, chans), F32)
    w_s[1, span : span + 8, :] = jnp.zeros((8, chans), F32)

    def input_gradient(d, carry):
        for t in range(chans // LANES):
            some = slice(t * LANES, (t + 1) * LANES)
            at = pl.ds(pl.multiple_of(d * chans + t * LANES, LANES), LANES)
            tap = [tap_s[i : i + 1, at] for i in range(9)]
            for c in reversed(range(chunks)):
                low = c * ROWS
                rows = slice(low, low + ROWS)
                back = back_s[rows, at]
                grads = [cot_ref[rows, at].astype(F32) * conv_s[rows, at], back * value_s[rows, at], back * key_s[rows, at]]
                ahead_by = [tap[j] * grads[0] + tap[3 + j] * grads[1] + tap[6 + j] * grads[2] for j in range(3)]
                w_s[0, rows, some] = ahead_by[1]
                w_s[1, rows, some] = ahead_by[2]
                part = (
                    ahead_by[0]
                    + w_s[0, low + 1 : low + 1 + ROWS, some]
                    + w_s[1, low + 2 : low + 2 + ROWS, some]
                )
                if c < chunks - 1:
                    grad_ref[rows, at] = part.astype(BF16)
                else:
                    tail_s[:, at] = part
            edge_stage[0:1, at] = w_s[1, 0:1, some]
            edge_stage[1:2, at] = w_s[0, 0:1, some] + w_s[1, 1:2, some]
        return carry

    lax.fori_loop(0, n, input_gradient, 0)
    edge = to_ctx(edge_stage, edge_recv, edge_sem.at[2], edge_sem.at[3], behind)
    edge.start()
    body = pl.ds(0, span - ROWS)
    main = pltpu.make_async_copy(grad_ref.at[body, :], grad_hbm.at[body, :], out_sem.at[0])
    main.start()

    edge.wait()
    tail_s[ROWS - 2 :, :] = tail_s[ROWS - 2 :, :] + jnp.where(me < n - 1, edge_recv[...], 0.0)
    grad_ref[span - ROWS :, :] = tail_s[...].astype(BF16)
    last = pl.ds(span - ROWS, ROWS)
    tail = pltpu.make_async_copy(grad_ref.at[last, :], grad_hbm.at[last, :], out_sem.at[1])
    tail.start()

    take_far(mode_two, mt_send, mt_sem)
    mode_three[mine] = sum_of(mode_two)
    send_near(lambda p: mode_three.at[mine], mode_three, mh_send, mh_sem)
    take_far(tap_far, tf_send, tf_sem)
    tap_near[mine] = packed(sum_of(tap_far))
    for copy, _ in around:
        copy().start()
    main.wait()
    tail.wait()
    take_near(mode_three, mh_send, mh_sem)
    for index in tiles:
        which, row, lane, slot, place = tile_of(index)
        row = PIECE + which * MODES + row
        total_ref[row : row + 8, lane : lane + LANES] = mode_three[slot, place : place + 8, :]
    for _, copy in around:
        copy().wait()
    total = tap_near[0].astype(F32)
    for p in range(1, near):
        total = total + tap_near[p].astype(F32)
    total_ref[:PIECE, :] = unpacked(total)


def hand_out(total_ref, grad_ref, grad_out, taps_out, table_out, res_out, decay_out):
    grad_out[...] = grad_ref[...]
    for s in range(3):
        table_out[s] = total_ref[4 * s : 4 * s + 4, :]
        taps_out[s] = total_ref[12 + 3 * s : 15 + 3 * s, :]
    res_out[...] = total_ref[PIECE : PIECE + MODES, :]
    decay_out[...] = total_ref[PIECE + MODES :, :]


def shards(n, near, groups, inputs, letters, letter_table, short_taps, residues, decay_rate, cotangent):
    span, width = inputs.shape[1:]
    chans = width // n
    wide = 4 if n % 8 == 0 else 2
    fixed = tables(span)
    nodes = fixed["nodes"]
    node_cols = np.broadcast_to(nodes[:, None], (NODES, chans)).astype(np.float32)
    vmem = pl.BlockSpec(memory_space=pltpu.VMEM)
    anywhere = pl.BlockSpec(memory_space=pl.ANY)
    dma = pltpu.SemaphoreType.DMA
    operands = [inputs[0], letters, letter_table, short_taps, residues.T, decay_rate.T, cotangent[0]] + [
        jnp.asarray(fixed[name]) for name in ("forward", "moments", "inverse", "spread", "response")
    ] + [jnp.asarray(node_cols)]
    several = wide * chans
    share = GRADS * chans // LANES // near
    scratch = [pltpu.VMEM(value.shape, value.dtype) for value in operands] + [
        pltpu.VMEM((ROWS, width), BF16),
        pltpu.VMEM((span + 2 * NODES, 2 * span), BF16),
        pltpu.VMEM((span, width), BF16),
        pltpu.VMEM((span + 8, width), F32),
        pltpu.VMEM((span, width), F32),
        pltpu.VMEM((span, width), F32),
        pltpu.VMEM((span, width), BF16),
        pltpu.VMEM((span, width), BF16),
        pltpu.VMEM((span, width), F32),
        pltpu.VMEM((span, width), F32),
        pltpu.VMEM((span, LANES), F32),
        pltpu.VMEM((ROWS, 3 * span), BF16),
        pltpu.VMEM((ROWS, width), F32),
        pltpu.VMEM((ROWS, width), F32),
        pltpu.VMEM((2 * span, width), F32),
        pltpu.VMEM((2 * span, width), F32),
        pltpu.VMEM((2 * span, width), F32),
        pltpu.VMEM((2, 2 * span, width), BF16),
        pltpu.VMEM((2, span, width), F32),
        pltpu.VMEM((3 * span, several), BF16),
        pltpu.VMEM((wide, PIECE, chans), F32),
        pltpu.VMEM((2, span + 8, chans), F32),
        pltpu.VMEM((ROWS, width), F32),
    ] + [pltpu.VMEM((NODES, MODES, chans), F32)] * 4 + [pltpu.VMEM((n, MODES, chans), F32)] * 6 + [
        pltpu.VMEM((2, 2 * NODES, chans), F32),
        pltpu.VMEM((2, MODES, chans), F32),
    ] + [pltpu.VMEM((2, width), F32)] * 4 + [
        pltpu.VMEM((NODES, chans), BF16),
        pltpu.VMEM((n, NODES, chans), BF16),
        pltpu.VMEM((n, 2 * NODES, chans), BF16),
        pltpu.VMEM((n, 2 * NODES, chans), BF16),
        pltpu.VMEM((n, NODES, chans), F32),
        pltpu.VMEM((n, NODES, chans), F32),
        pltpu.VMEM((n, 2 * NODES, chans), BF16),
        pltpu.VMEM((n, 2 * NODES, chans), BF16),
        pltpu.VMEM((n, 16, chans * 3 // 2), BF16),
        pltpu.VMEM((n, 16, chans * 3 // 2), BF16),
        pltpu.VMEM((near, share, LANES), F32),
        pltpu.VMEM((near, share, LANES), F32),
        pltpu.VMEM((groups, share, LANES), F32),
        pltpu.VMEM((near, share, LANES), F32),
        pltpu.VMEM((near, 16, chans * 3 // 2), BF16),
        pltpu.VMEM((groups, PIECE, chans), F32),
        dma((len(operands) + 1,)),
        dma((2,)),
        dma((4,)),
    ] + [dma((n,))] * 10 + ([dma((near,))] * 2 + [dma((groups,))] * 2 + [dma((near,))] * 2) + [dma((near,))] * 2 + [dma((groups,))] * 2
    grad, total = pl.pallas_call(
        functools.partial(kernel, n, near, groups, wide, span, chans, nodes),
        out_shape=(
            jax.ShapeDtypeStruct((span, width), BF16),
            jax.ShapeDtypeStruct((PIECE + GRADS, chans), F32),
        ),
        in_specs=[anywhere] * len(operands),
        out_specs=(anywhere, vmem),
        scratch_shapes=scratch,
        compiler_params=pltpu.CompilerParams(
            collective_id=0, has_side_effects=True, vmem_limit_bytes=56 * 1024 * 1024
        ),
    )(*operands)
    grad, taps_grad, table_grad, residue_grad, decay_grad = pl.pallas_call(
        hand_out,
        out_shape=(
            jax.ShapeDtypeStruct((span, width), BF16),
            jax.ShapeDtypeStruct((3, 3, chans), F32),
            jax.ShapeDtypeStruct((3, 4, chans), F32),
            jax.ShapeDtypeStruct((MODES, chans), F32),
            jax.ShapeDtypeStruct((MODES, chans), F32),
        ),
        in_specs=[vmem] * 2,
        out_specs=(vmem,) * 5,
        compiler_params=pltpu.CompilerParams(vmem_limit_bytes=56 * 1024 * 1024),
    )(total, grad)
    return grad[None], taps_grad, table_grad, residue_grad.T, decay_grad.T


def solution(mesh):
    n, sequences = mesh.shape["ctx"], mesh.shape["dp"]
    near = max(k for k in (1, 2, 4, 8) if sequences % k == 0 and k * k <= 2 * sequences)
    in_specs = (
        P("dp", "ctx", None),
        P("dp", "ctx"),
        P(),
        P(),
        P("ctx", None),
        P("ctx", None),
        P("dp", "ctx", None),
    )
    out_specs = (
        P("dp", "ctx", None),
        P(None, None, "ctx"),
        P(None, None, "ctx"),
        P("ctx", None),
        P("ctx", None),
    )
    body = functools.partial(shards, n, near, sequences // near)
    return jax.shard_map(body, mesh=mesh, in_specs=in_specs, out_specs=out_specs, check_vma=False)
```
